512 devices in a mesh: row: 32 (over x, z_lo, core), ch: 16 (over y, z_hi).
Axes of the slice: x: 4, y: 8, z: 8 (z_hi: 2, z_lo: 4; z = z_hi * 4 + z_lo), core: 2. Of those that a mesh axis runs over, the one named last changes fastest.
Arguments:
- pair: float32 [512, 512, 128], P('row', 'ch'), may hold values from -6 to 6
- out_inputs: bfloat16 [128, 512], replicated, may hold values from -0.5 to 0.5
- out_gate: bfloat16 [128, 128], replicated, may hold values from -0.5 to 0.5
- out_final: bfloat16 [128, 128], replicated, may hold values from -0.5 to 0.5
- in_inputs: bfloat16 [128, 512], replicated, may hold values from -0.5 to 0.5
- in_gate: bfloat16 [128, 128], replicated, may hold values from -0.5 to 0.5
- in_final: bfloat16 [128, 128], replicated, may hold values from -0.5 to 0.5
Outputs:
- updated: float32 [512, 512, 128], P('row', 'ch')
The draws below stay inside these ranges and needn't reach their ends.
All inputs are finite; a program needn't handle non-finite values.
Results may differ from the reference program's by a relative error of at most 0.0065.
Values may be sent and summed in bfloat16 or wider, within the bound.
A program may use at most 64 MiB of HBM per device.

```python
import jax
import jax.numpy as jnp
from jax import lax

C = 128
H = 128
RES = 512


def steps_of(stream_key, extent, cuts, low, largest):
    def one(dim, shards_of):
        draws = jax.random.uniform(jax.random.fold_in(jax.random.fold_in(stream_key, 6), dim), (shards_of,), jnp.float32, low / len(cuts), largest / len(cuts))
        return jnp.repeat(jnp.exp(draws), extent[dim] // shards_of).reshape((-1,) + (1,) * (len(extent) - dim - 1))

    factor_of = one(*cuts[0])
    for cut in cuts[1:]:
        factor_of = factor_of * one(*cut)
    return factor_of


def bell_draw(own_key, extent, scale, reach, pieces=(), held_as=jnp.bfloat16):
    loudness = steps_of(own_key, extent, pieces, -0.22, 0.18) if pieces else 1.0
    result = jax.random.normal(own_key, extent, jnp.float32) * scale * loudness
    return jnp.minimum(jnp.maximum(result, -reach), reach).astype(held_as)


def setup_inputs(seed: int = 0) -> dict:
    splits = jax.random.split(jax.random.key(seed), 8)
    pair = bell_draw(splits[0], (RES, RES, C), 1.0, 6.0, ((0, 32), (1, 16)), jnp.float32)
    out_inputs = bell_draw(splits[1], (C, 4 * H), C ** -0.5, 0.5)
    out_gate = bell_draw(splits[2], (C, C), C ** -0.5, 0.5)
    out_final = bell_draw(splits[3], (H, C), H ** -0.5, 0.5)
    in_inputs = bell_draw(splits[4], (C, 4 * H), C ** -0.5, 0.5)
    in_gate = bell_draw(splits[5], (C, C), C ** -0.5, 0.5)
    in_final = bell_draw(splits[6], (H, C), H ** -0.5, 0.5)
    return {"pair": pair, "out_inputs": out_inputs, "out_gate": out_gate, "out_final": out_final, "in_inputs": in_inputs, "in_gate": in_gate, "in_final": in_final}


def normalize(values):
    mean = lax.optimization_barrier(jnp.mean(values, axis=-1, keepdims=True))
    centered = values - mean
    variance = lax.optimization_barrier(jnp.mean(centered * centered, axis=-1, keepdims=True))
    return centered / jnp.sqrt(variance + 1e-05)

def triangle(field, w_inputs, w_gate, w_final, outgoing):
    width = w_final.shape[0]
    chans = field.shape[2]
    normed = normalize(field).astype(jnp.bfloat16)
    flat = normed.reshape(-1, chans)
    proj = jnp.dot(flat, w_inputs, preferred_element_type=jnp.float32).reshape(RES, RES, 4 * width)
    left = (jax.nn.sigmoid(proj[..., width:2 * width]) * proj[..., :width]).astype(jnp.bfloat16)
    right = (jax.nn.sigmoid(proj[..., 3 * width:]) * proj[..., 2 * width:3 * width]).astype(jnp.bfloat16)
    left_full = left.astype(jnp.float32)
    right_full = right.astype(jnp.float32)
    if outgoing:
        product = jnp.einsum('ikc,jkc->ijc', left_full, right_full)
    else:
        product = jnp.einsum('kic,kjc->ijc', left_full, right_full)
    product_normed = normalize(product).astype(jnp.bfloat16)
    update = jnp.dot(product_normed.reshape(-1, width), w_final, preferred_element_type=jnp.float32).reshape(RES, RES, chans)
    gating = jax.nn.sigmoid(jnp.dot(flat, w_gate, preferred_element_type=jnp.float32).reshape(RES, RES, chans))
    return field + gating * update

def reference(pair, out_inputs, out_gate, out_final, in_inputs, in_gate, in_final):
    middle = triangle(pair, out_inputs, out_gate, out_final, True)
    return triangle(middle, in_inputs, in_gate, in_final, False)
```

```python
import jax
import jax.numpy as jnp
from jax import lax
from jax.experimental import pallas as pl
from jax.experimental.pallas import tpu as pltpu
from jax.sharding import PartitionSpec as P

MESH = pl.DeviceIdType.MESH
BF16 = jnp.bfloat16
F32 = jnp.float32
Y = 8
ROWS = 32
OWNERS = 16
PHASES = 10


def norm0(values):
    mean = jnp.mean(values, axis=0, keepdims=True)
    centered = values - mean
    variance = jnp.mean(centered * centered, axis=0, keepdims=True)
    return centered * lax.rsqrt(variance + 1e-05)


def flip(w):
    return w.astype(F32).T.astype(BF16)


def place(row):
    return pl.multiple_of((row // 2 % 2) * 256 + (row // 4) * 32 + (row % 2) * 16, 16)


def owner_row(m):
    x = m // 4
    return x * 8 + (2 * (m % 2) + x % 2) * 2


def owner_half(m):
    return m % 4 // 2


def kernel(
    z_ref, wi0, wg0, wf0, wi1, wg1, wf1, u_ref,
    z_send, z_got, wi_t, wg_t, wf_t, zt, acc, gate,
    b1_send, b1_got, turn, b2_send, operands, x_send, c1_got, c2_send, c2_got,
    u_send, u_got, size63, send_sem, recv_sem,
):
    row = lax.axis_index("row")
    ch = lax.axis_index("ch")
    y = ch // 2
    half = ch % 2
    x_pos, zlo = row // 8, row % 8 // 2
    mine = x_pos * 4 + half * 2 + zlo // 2
    is_owner = jnp.logical_and(row % 2 == 0, zlo % 2 == x_pos % 2)
    slot = row * 2 + half

    def send(phase, src, dst, to_row, to_ch):
        pltpu.make_async_remote_copy(
            src_ref=src, dst_ref=dst, send_sem=send_sem.at[phase], recv_sem=recv_sem.at[phase],
            device_id=(to_row, to_ch), device_id_type=MESH,
        ).start()

    def keep(phase, src, dst):
        pltpu.make_async_copy(src, dst, recv_sem.at[phase]).start()

    def arrive(phase, ref):
        pltpu.make_async_copy(ref, ref, recv_sem.at[phase]).wait()

    def leave(phase, ref):
        pltpu.make_async_copy(ref, ref, send_sem.at[phase]).wait()

    def over_y(phase, src_of, dst):
        for step in range(1, Y):
            peer = (y + step) % Y
            send(phase, src_of(peer), dst, row, peer * 2 + half)
        keep(phase, src_of(y), dst)

    def swap(src, dst_of):
        for part in range(2):
            lanes = slice(part * 128, part * 128 + 128)
            turn[part] = src[:, :, lanes].astype(F32).reshape(256, 128)
            for b in range(16):
                dst_of(b)[:, lanes] = turn.at[part][pl.ds(b, 16, stride=16), :].astype(BF16)

    barrier = pltpu.get_barrier_semaphore()

    def greet(to_row, to_ch):
        pl.semaphore_signal(barrier, inc=1, device_id=(to_row, to_ch), device_id_type=MESH)

    for step in range(1, Y):
        greet(row, (y + step) % Y * 2 + half)

    @pl.when(is_owner)
    def _():
        def one(step, carry):
            peer = (slot + step) % 64
            greet(peer // 2, y * 2 + peer % 2)
            return carry

        lax.fori_loop(1, 64, one, 0)

    @pl.when(jnp.logical_not(is_owner))
    def _():
        for m in range(OWNERS):
            greet(owner_row(m), y * 2 + owner_half(m))

    z_send[...] = z_ref[...].astype(BF16)

    @pl.when(is_owner)
    def _():
        pl.semaphore_wait(barrier, Y - 1 + 63)

    @pl.when(jnp.logical_not(is_owner))
    def _():
        pl.semaphore_wait(barrier, Y - 1 + OWNERS)

    over_y(
        0,
        lambda peer: z_send.at[pl.ds(peer * 2, 2)],
        z_got.at[:, pl.ds(pl.multiple_of(y * 32, 32), 32), :],
    )
    for u, (wi, wg, wf) in enumerate(((wi0, wg0, wf0), (wi1, wg1, wf1))):
        wi_t[u] = flip(wi[...])
        wg_t[u] = flip(wg[...])
        wf_t[u] = flip(wf[...])
    arrive(0, z_got)
    for i in range(2):
        zt[i] = z_got[i].astype(F32).T

    for u in range(2):
        b1, b2, c1, c2 = (1 + 4 * u + n for n in range(4))
        for i in range(2):
            zn = norm0(zt[i]).astype(BF16)
            proj = jnp.dot(wi_t[u], zn, preferred_element_type=F32)
            b1_send[u, 0, i] = (jax.nn.sigmoid(proj[128:256]) * proj[:128]).astype(BF16)
            b1_send[u, 1, i] = (jax.nn.sigmoid(proj[384:]) * proj[256:384]).astype(BF16)
            gate[i] = jax.nn.sigmoid(jnp.dot(wg_t[u], zn, preferred_element_type=F32))
        over_y(
            b1,
            lambda peer: b1_send.at[u, :, :, pl.ds(pl.multiple_of(peer * 16, 16), 16), :],
            b1_got.at[u, :, pl.ds(y * 2, 2)],
        )
        arrive(b1, b1_got.at[u])
        for side in range(2):
            swap(b1_got.at[u, side], lambda c: b2_send.at[u, c, side])

        here = operands.at[
            u, :, pl.ds(place(row), 16), pl.ds(pl.multiple_of(half * 256, 256), 256)
        ]

        def to_owner(step, carry):
            m = (slot + step) % OWNERS
            own = jnp.logical_and(is_owner, m == mine)

            @pl.when(own)
            def _():
                keep(b2, b2_send.at[u, m], here)

            @pl.when(jnp.logical_not(own))
            def _():
                send(b2, b2_send.at[u, m], here, owner_row(m), y * 2 + owner_half(m))

            return carry

        lax.fori_loop(0, OWNERS, to_owner, 0)

        @pl.when(is_owner)
        def _():
            arrive(b2, operands.at[u])

            def part(q, carry):
                rows = pl.ds(pl.multiple_of(q * 128, 128), 128)
                if u == 0:
                    product = lax.dot_general(
                        operands[u, 0, rows, :], operands[u, 1],
                        (((1,), (1,)), ((), ())), preferred_element_type=F32,
                    )
                else:
                    product = lax.dot_general(
                        operands[u, 0, :, rows], operands[u, 1],
                        (((0,), (0,)), ((), ())), preferred_element_type=F32,
                    )
                x_send[u, rows, :] = product.astype(BF16)
                return carry

            lax.fori_loop(0, 4, part, 0)

            def block(peer):
                return x_send.at[
                    u, pl.ds(place(peer // 2), 16),
                    pl.ds(pl.multiple_of(peer % 2 * 256, 256), 256),
                ]

            def back(step, carry):
                peer = (slot + step) % 64
                send(c1, block(peer), c1_got.at[u, mine], peer // 2, y * 2 + peer % 2)
                return carry

            keep(c1, block(slot), c1_got.at[u, mine])
            lax.fori_loop(1, 64, back, 0)

        arrive(c1, c1_got.at[u])
        swap(c1_got.at[u], lambda i: c2_send.at[u, i])
        over_y(
            c2,
            lambda peer: c2_send.at[u, pl.ds(peer * 2, 2)],
            c2_got.at[u, :, pl.ds(pl.multiple_of(y * 16, 16), 16), :],
        )
        arrive(c2, c2_got.at[u])
        for i in range(2):
            xn = norm0(c2_got[u, i].astype(F32)).astype(BF16)
            update = gate[i] * jnp.dot(wf_t[u], xn, preferred_element_type=F32)
            if u == 0:
                acc[i] = update
                zt[i] += update
            else:
                u_send[i] = (acc[i] + update).T.astype(BF16)

    over_y(
        9,
        lambda peer: u_send.at[:, pl.ds(pl.multiple_of(peer * 32, 32), 32), :],
        u_got.at[pl.ds(y * 2, 2)],
    )
    leave(0, z_send.at[pl.ds(0, 14)])
    for u in range(2):
        b1, b2, c1, c2 = (1 + 4 * u + n for n in range(4))
        leave(b1, b1_send.at[u, :, :, pl.ds(0, 112), :])

        @pl.when(is_owner)
        def _():
            leave(b2, b2_send.at[u, pl.ds(0, 15)])
            leave(c1, size63)

        @pl.when(jnp.logical_not(is_owner))
        def _():
            leave(b2, b2_send.at[u])

        leave(c2, c2_send.at[u, pl.ds(0, 14)])
    leave(9, u_send.at[:, pl.ds(0, 224), :])
    arrive(9, u_got)
    u_ref[...] = u_got[...]


def body(pair, out_inputs, out_gate, out_final, in_inputs, in_gate, in_final):
    vmem = pl.BlockSpec(memory_space=pltpu.VMEM)
    total = pl.pallas_call(
        kernel,
        out_shape=jax.ShapeDtypeStruct((16, 32, 128), BF16),
        in_specs=[vmem] * 7,
        out_specs=vmem,
        scratch_shapes=[
            pltpu.VMEM((16, 32, 128), BF16),
            pltpu.VMEM((2, 256, 128), BF16),
            pltpu.VMEM((2, 512, 128), BF16),
            pltpu.VMEM((2, 128, 128), BF16),
            pltpu.VMEM((2, 128, 128), BF16),
            pltpu.VMEM((2, 128, 256), F32),
            pltpu.VMEM((2, 128, 256), F32),
            pltpu.VMEM((2, 128, 256), F32),
            pltpu.VMEM((2, 2, 2, 128, 256), BF16),
            pltpu.VMEM((2, 2, 16, 16, 256), BF16),
            pltpu.VMEM((2, 256, 128), F32),
            pltpu.VMEM((2, 16, 2, 16, 256), BF16),
            pltpu.VMEM((2, 2, 512, 512), BF16),
            pltpu.VMEM((2, 512, 512), BF16),
            pltpu.VMEM((2, 16, 16, 256), BF16),
            pltpu.VMEM((2, 16, 16, 256), BF16),
            pltpu.VMEM((2, 2, 128, 256), BF16),
            pltpu.VMEM((2, 256, 128), BF16),
            pltpu.VMEM((16, 32, 128), BF16),
            pltpu.VMEM((1008, 256), BF16),
            pltpu.SemaphoreType.DMA((PHASES,)),
            pltpu.SemaphoreType.DMA((PHASES,)),
        ],
        compiler_params=pltpu.CompilerParams(
            collective_id=0, has_side_effects=True, vmem_limit_bytes=40 * 1024 * 1024
        ),
        name="triangles",
    )(pair, out_inputs, out_gate, out_final, in_inputs, in_gate, in_final)
    return pair + total.astype(F32)


def solution(mesh):
    placed = (P("row", "ch", None), P(), P(), P(), P(), P(), P())
    return jax.shard_map(
        body, mesh=mesh, in_specs=placed, out_specs=P("row", "ch", None), check_vma=False
    )
```

```python
import jax
import jax.numpy as jnp
from jax import lax
from jax.experimental import pallas as pl
from jax.experimental.pallas import tpu as pltpu
from jax.sharding import PartitionSpec as P

MESH = pl.DeviceIdType.MESH
BF16 = jnp.bfloat16
F32 = jnp.float32
GROUP = 8
OWNERS = 16
PHASES = 10


def norm0(values):
    mean = jnp.mean(values, axis=0, keepdims=True)
    centered = values - mean
    variance = jnp.mean(centered * centered, axis=0, keepdims=True)
    return centered * lax.rsqrt(variance + 1e-05)


def flip(w):
    return w.astype(F32).T.astype(BF16)


def place(zlo, y):
    return pl.multiple_of(zlo * 128 + y * 16, 16)


def runs(chunk):
    for y in range(chunk, 8, 2):
        for high in range(2):
            for low in range(2):
                yield y * 32 + high * 16 + low, y // 2 * 4 + high * 2 + low


def kernel(
    z_hbm, wi0, wg0, wf0, wi1, wg1, wf1, u_ref,
    z_in, wi_in, wg_in, wf_in, z_send, z_got, wi_t, wg_t, wf_t, zt, acc, gate,
    b1_send, b1_got, natural_rows, ordered_rows, turn, b2_send, operands, x_send,
    c1_got, c2_send, c2_got, u_send, u_got, size63, send_sem, recv_sem, in_sem,
):
    row = lax.axis_index("row")
    ch = lax.axis_index("ch")
    y, zhi = ch // 2, ch % 2
    x, zlo, core = row // 8, row % 8 // 2, row % 2
    g = x * 2 + core

    def owner_zlo(m):
        return m // 2 % 2 + 2 * ((m // 4 + core) % 2)

    def plane(peer_zlo):
        return x * 8 + peer_zlo * 2 + core

    is_owner = zlo == owner_zlo(ch)

    def send(phase, chunk, src, dst, to_row, to_ch):
        pltpu.make_async_remote_copy(
            src_ref=src, dst_ref=dst,
            send_sem=send_sem.at[phase], recv_sem=recv_sem.at[phase, chunk],
            device_id=(to_row, to_ch), device_id_type=MESH,
        ).start()

    def keep(phase, chunk, src, dst):
        pltpu.make_async_copy(src, dst, recv_sem.at[phase, chunk]).start()

    def arrive(phase, chunk, ref):
        pltpu.make_async_copy(ref, ref, recv_sem.at[phase, chunk]).wait()

    def leave(phase, ref):
        pltpu.make_async_copy(ref, ref, send_sem.at[phase]).wait()

    def y_peer(step):
        peer = (y + step) % GROUP
        return peer, row, peer * 2 + zhi

    def g_peer(step):
        peer = (g + step) % GROUP
        return peer, peer // 2 * 8 + zlo * 2 + peer % 2, ch

    def z_peer(step):
        peer = (zhi * 4 + zlo + step) % GROUP
        return peer, plane(peer % 4), y * 2 + peer // 4

    def spread(phase, chunk, peer_of, src_of, dst):
        for step in range(1, GROUP):
            peer, to_row, to_ch = peer_of(step)
            send(phase, chunk, src_of(peer), dst, to_row, to_ch)
        keep(phase, chunk, src_of(peer_of(0)[0]), dst)

    def swap(src, dst_of):
        turn[...] = src[...].astype(F32).reshape(256, 128)
        for b in range(16):
            dst_of(b)[...] = turn[pl.ds(b, 16, stride=16), :].astype(BF16)

    weights = ((wi0, wi_in.at[0]), (wg0, wg_in.at[0]), (wf0, wf_in.at[0]),
               (wi1, wi_in.at[1]), (wg1, wg_in.at[1]), (wf1, wf_in.at[1]))
    loads = [
        pltpu.make_async_copy(src, dst, in_sem.at[n])
        for n, (src, dst) in enumerate(((z_hbm, z_in), *weights))
    ]
    for load in loads:
        load.start()

    barrier = pltpu.get_barrier_semaphore()
    for line in (y_peer, g_peer, z_peer):
        for step in range(1, GROUP):
            _, to_row, to_ch = line(step)
            pl.semaphore_signal(
                barrier, inc=1, device_id=(to_row, to_ch), device_id_type=MESH
            )
    loads[0].wait()
    z_send[...] = z_in[...].astype(BF16)
    pl.semaphore_wait(barrier, 3 * (GROUP - 1))

    spread(
        0, 0, y_peer,
        lambda peer: z_send.at[pl.ds(peer * 2, 2)],
        z_got.at[:, pl.ds(pl.multiple_of(y * 32, 32), 32), :],
    )
    for load in loads[1:]:
        load.wait()
    for u in range(2):
        wi_t[u] = flip(wi_in[u])
        wg_t[u] = flip(wg_in[u])
        wf_t[u] = flip(wf_in[u])
    arrive(0, 0, z_got)

    def project(u, chunk, field):
        zn = norm0(field).astype(BF16)
        proj = jnp.dot(wi_t[u], zn, preferred_element_type=F32)
        left = (jax.nn.sigmoid(proj[128:256]) * proj[:128]).astype(BF16)
        right = (jax.nn.sigmoid(proj[384:]) * proj[256:384]).astype(BF16)
        for i in range(2):
            b1_send[u, chunk, 0, i] = left[:, i * 128:i * 128 + 128]
            b1_send[u, chunk, 1, i] = right[:, i * 128:i * 128 + 128]
        spread(
            1 + 4 * u, chunk, g_peer,
            lambda peer: b1_send.at[
                u, chunk, :, :, pl.ds(pl.multiple_of(peer * 16, 16), 16), :
            ],
            b1_got.at[u, chunk, :, pl.ds(g * 2, 2)],
        )
        gate[chunk] = jax.nn.sigmoid(jnp.dot(wg_t[u], zn, preferred_element_type=F32))

    for chunk in range(2):
        for i in range(2):
            natural_rows[...] = z_got[i].astype(F32)
            for natural, ordered in runs(chunk):
                ordered_rows[pl.ds(ordered, 8, stride=16), :] = natural_rows[
                    pl.ds(natural, 8, stride=2), :
                ]
            zt[chunk, :, i * 128:i * 128 + 128] = ordered_rows[...].T
        project(0, chunk, zt[chunk])

    for u in range(2):
        b1, b2, c1, c2 = (1 + 4 * u + n for n in range(4))
        for chunk in range(2):
            arrive(b1, chunk, b1_got.at[u, chunk])
            for side in range(2):
                swap(b1_got.at[u, chunk, side], lambda c: b2_send.at[u, chunk, c, side])
            here = operands.at[
                u, :, pl.ds(place(zlo, y), 16),
                pl.ds(pl.multiple_of(chunk * 256 + zhi * 128, 128), 128),
            ]
            for step in range(1, OWNERS):
                m = (ch + step) % OWNERS
                send(b2, chunk, b2_send.at[u, chunk, m], here, plane(owner_zlo(m)), m)

            @pl.when(is_owner)
            def _():
                keep(b2, chunk, b2_send.at[u, chunk, ch], here)

            @pl.when(jnp.logical_not(is_owner))
            def _():
                send(b2, chunk, b2_send.at[u, chunk, ch], here, plane(owner_zlo(ch)), ch)

        @pl.when(is_owner)
        def _():
            for chunk in range(2):
                arrive(b2, chunk, operands.at[u, :, :, pl.ds(chunk * 256, 256)])
            for chunk in range(2):
                mine = c1_got.at[u, chunk, ch]

                def back(step, carry):
                    peer_zlo = (zlo + step) % 4
                    rows = pl.ds(pl.multiple_of(peer_zlo * 128, 128), 128)
                    columns = pl.ds(chunk * 256, 256)
                    if u == 0:
                        product = lax.dot_general(
                            operands[u, 0, rows, :], operands[u, 1, columns, :],
                            (((1,), (1,)), ((), ())), preferred_element_type=F32,
                        )
                    else:
                        product = lax.dot_general(
                            operands[u, 0, :, rows], operands[u, 1, :, columns],
                            (((0,), (0,)), ((), ())), preferred_element_type=F32,
                        )
                    x_send[u, chunk, rows, :] = product.astype(BF16)

                    def block(peer_ch):
                        return x_send.at[
                            u, chunk, pl.ds(place(peer_zlo, peer_ch // 2), 16),
                            pl.ds(pl.multiple_of(peer_ch % 2 * 128, 128), 128),
                        ]

                    for other in range(1, 16):
                        peer_ch = (ch + other) % 16
                        send(c1, chunk, block(peer_ch), mine, plane(peer_zlo), peer_ch)

                    @pl.when(peer_zlo == zlo)
                    def _():
                        keep(c1, chunk, block(ch), mine)

                    @pl.when(peer_zlo != zlo)
                    def _():
                        send(c1, chunk, block(ch), mine, plane(peer_zlo), ch)

                    return carry

                lax.fori_loop(1, 5, back, 0)

        for chunk in range(2):
            arrive(c1, chunk, c1_got.at[u, chunk])
            swap(c1_got.at[u, chunk], lambda i: c2_send.at[u, chunk, i])
            spread(
                c2, chunk, g_peer,
                lambda peer: c2_send.at[u, chunk, pl.ds(peer * 2, 2)],
                c2_got.at[u, chunk, :, pl.ds(pl.multiple_of(g * 16, 16), 16), :],
            )
        for chunk in range(2):
            arrive(c2, chunk, c2_got.at[u, chunk])
            product = jnp.concatenate(
                [c2_got[u, chunk, i].astype(F32) for i in range(2)], axis=1
            )
            update = gate[chunk] * jnp.dot(
                wf_t[u], norm0(product).astype(BF16), preferred_element_type=F32
            )
            if u == 0:
                acc[chunk] = update
                project(1, chunk, zt[chunk] + update)
                continue
            total = acc[chunk] + update
            for i in range(2):
                ordered_rows[...] = total[:, i * 128:i * 128 + 128].T
                for natural, ordered in runs(chunk):
                    natural_rows[pl.ds(natural, 8, stride=2), :] = ordered_rows[
                        pl.ds(ordered, 8, stride=16), :
                    ]
                for part in range(chunk, 8, 2):
                    there = slice(part * 32, part * 32 + 32)
                    u_send[i, there, :] = natural_rows[there, :].astype(BF16)
            home = u_got.at[pl.ds(y * 2, 2)]

            def columns_of(peer):
                return u_send.at[:, pl.ds(pl.multiple_of(peer * 32, 32), 32), :]

            for step in range(1, 4):
                peer = (y // 2 + step) % 4 * 2 + chunk
                send(9, 0, columns_of(peer), home, row, peer * 2 + zhi)

            @pl.when(y % 2 == chunk)
            def _():
                keep(9, 0, columns_of(y), home)

            @pl.when(y % 2 != chunk)
            def _():
                peer = y // 2 * 2 + chunk
                send(9, 0, columns_of(peer), home, row, peer * 2 + zhi)

    leave(0, z_send.at[pl.ds(0, 14)])
    for u in range(2):
        b1, b2, c1, c2 = (1 + 4 * u + n for n in range(4))
        leave(b1, b1_send.at[u, :, :, :, pl.ds(0, 112), :])

        @pl.when(is_owner)
        def _():
            leave(b2, b2_send.at[u, :, pl.ds(0, 15)])
            leave(c1, size63)

        @pl.when(jnp.logical_not(is_owner))
        def _():
            leave(b2, b2_send.at[u])

        leave(c2, c2_send.at[u, :, pl.ds(0, 14)])
    leave(9, u_send.at[:, pl.ds(0, 224), :])
    arrive(9, 0, u_got)
    u_ref[...] = u_got[...]


def body(pair, out_inputs, out_gate, out_final, in_inputs, in_gate, in_final):
    anywhere = pl.BlockSpec(memory_space=pl.ANY)
    total = pl.pallas_call(
        kernel,
        out_shape=jax.ShapeDtypeStruct((16, 32, 128), BF16),
        in_specs=[anywhere] * 7,
        out_specs=pl.BlockSpec(memory_space=pltpu.VMEM),
        scratch_shapes=[
            pltpu.VMEM((16, 32, 128), F32),
            pltpu.VMEM((2, 128, 512), BF16),
            pltpu.VMEM((2, 128, 128), BF16),
            pltpu.VMEM((2, 128, 128), BF16),
            pltpu.VMEM((16, 32, 128), BF16),
            pltpu.VMEM((2, 256, 128), BF16),
            pltpu.VMEM((2, 512, 128), BF16),
            pltpu.VMEM((2, 128, 128), BF16),
            pltpu.VMEM((2, 128, 128), BF16),
            pltpu.VMEM((2, 128, 256), F32),
            pltpu.VMEM((2, 128, 256), F32),
            pltpu.VMEM((2, 128, 256), F32),
            pltpu.VMEM((2, 2, 2, 2, 128, 128), BF16),
            pltpu.VMEM((2, 2, 2, 16, 16, 128), BF16),
            pltpu.VMEM((256, 128), F32),
            pltpu.VMEM((128, 128), F32),
            pltpu.VMEM((256, 128), F32),
            pltpu.VMEM((2, 2, 16, 2, 16, 128), BF16),
            pltpu.VMEM((2, 2, 512, 512), BF16),
            pltpu.VMEM((2, 2, 512, 256), BF16),
            pltpu.VMEM((2, 2, 16, 16, 128), BF16),
            pltpu.VMEM((2, 2, 16, 16, 128), BF16),
            pltpu.VMEM((2, 2, 2, 128, 128), BF16),
            pltpu.VMEM((2, 256, 128), BF16),
            pltpu.VMEM((16, 32, 128), BF16),
            pltpu.VMEM((1008, 256), BF16),
            pltpu.SemaphoreType.DMA((PHASES,)),
            pltpu.SemaphoreType.DMA((PHASES, 2)),
            pltpu.SemaphoreType.DMA((7,)),
        ],
        compiler_params=pltpu.CompilerParams(
            collective_id=0, has_side_effects=True, vmem_limit_bytes=60 * 1024 * 1024
        ),
        name="triangles",
    )(pair, out_inputs, out_gate, out_final, in_inputs, in_gate, in_final)
    return pair + total.astype(F32)


def solution(mesh):
    placed = (P("row", "ch", None), P(), P(), P(), P(), P(), P())
    return jax.shard_map(
        body, mesh=mesh, in_specs=placed, out_specs=P("row", "ch", None), check_vma=False
    )
```

```python
import jax
import jax.numpy as jnp
from jax import lax
from jax.experimental import pallas as pl
from jax.experimental.pallas import tpu as pltpu
from jax.sharding import PartitionSpec as P

MESH = pl.DeviceIdType.MESH
BF16 = jnp.bfloat16
F32 = jnp.float32
GROUP = 8
OWNERS = 16
FAR_FIRST = (4, 3, 5, 2, 6, 1, 7)
PHASES = 10


def norm0(values):
    mean = jnp.mean(values, axis=0, keepdims=True)
    centered = values - mean
    variance = jnp.mean(centered * centered, axis=0, keepdims=True)
    return centered * lax.rsqrt(variance + 1e-05)


def flip(w):
    return w.astype(F32).T.astype(BF16)


def place(zlo, y):
    return pl.multiple_of(zlo * 128 + y * 16, 16)


def kernel(
    z_hbm, wi0, wg0, wf0, wi1, wg1, wf1, out_ref,
    z_in, wi_in, wg_in, wf_in, z_send, z_got, wi_t, wg_t, wf_t, zt, acc, gate,
    h_send, h_got, fan, square, k_send, b1_send, b1_got, turn, b2_send, operands,
    x1_send, c1_got, c2_send, c2_got, x2_send, t1_got, t2_send, t2_got,
    u_send, u_got, middle_t, home_gate, turned, size63, send_sem, recv_sem, in_sem, ready,
):
    row = lax.axis_index("row")
    ch = lax.axis_index("ch")
    y, zhi = ch // 2, ch % 2
    x, zlo, core = row // 8, row % 8 // 2, row % 2
    g = x * 2 + core

    def owner_zlo(m):
        return m // 2 % 2 + 2 * ((m // 4 + core) % 2)

    def plane(peer_zlo):
        return x * 8 + peer_zlo * 2 + core

    is_owner = zlo == owner_zlo(ch)

    def send(phase, chunk, src, dst, to_row, to_ch):
        pltpu.make_async_remote_copy(
            src_ref=src, dst_ref=dst,
            send_sem=send_sem.at[phase], recv_sem=recv_sem.at[phase, chunk],
            device_id=(to_row, to_ch), device_id_type=MESH,
        ).start()

    def keep(phase, chunk, src, dst):
        pltpu.make_async_copy(src, dst, recv_sem.at[phase, chunk]).start()

    def arrive(phase, chunk, ref):
        pltpu.make_async_copy(ref, ref, recv_sem.at[phase, chunk]).wait()

    def leave(phase, ref):
        pltpu.make_async_copy(ref, ref, send_sem.at[phase]).wait()

    def y_peer(step):
        peer = (y + step) % GROUP
        return peer, row, peer * 2 + zhi

    def g_peer(step):
        peer = (g + step) % GROUP
        return peer, peer // 2 * 8 + zlo * 2 + peer % 2, ch

    def z_peer(step):
        peer = (zhi * 4 + zlo + step) % GROUP
        return peer, plane(peer % 4), y * 2 + peer // 4

    def spread(phase, chunk, peer_of, src_of, dst):
        for step in FAR_FIRST:
            peer, to_row, to_ch = peer_of(step)
            send(phase, chunk, src_of(peer), dst, to_row, to_ch)
        keep(phase, chunk, src_of(peer_of(0)[0]), dst)

    def others():
        for dy in (*FAR_FIRST, 0):
            for dz in (1, 0):
                if dy or dz:
                    yield (y + dy) % 8 * 2 + (zhi + dz) % 2

    def to_owners(phase, chunk, src_of, here):
        for m in others():
            send(phase, chunk, src_of(m), here, plane(owner_zlo(m)), m)

        @pl.when(is_owner)
        def _():
            keep(phase, chunk, src_of(ch), here)

        @pl.when(jnp.logical_not(is_owner))
        def _():
            send(phase, chunk, src_of(ch), here, plane(owner_zlo(ch)), ch)

    def both(stage):
        def one(chunk, carry):
            stage(chunk)
            return carry

        lax.fori_loop(0, 2, one, 0)

    def swap(src, dst_of):
        turn[...] = src[...].astype(F32).reshape(256, 128)
        for b in range(16):
            dst_of(b)[...] = turn[pl.ds(b, 16, stride=16), :].astype(BF16)

    def lanes(n, width=128):
        return slice(n * width, (n + 1) * width)

    def glu(proj):
        return (jax.nn.sigmoid(proj[128:]) * proj[:128]).astype(BF16)

    weights = ((wi0, wi_in.at[0]), (wg0, wg_in.at[0]), (wf0, wf_in.at[0]),
               (wi1, wi_in.at[1]), (wg1, wg_in.at[1]), (wf1, wf_in.at[1]))
    loads = [
        pltpu.make_async_copy(src, dst, in_sem.at[n])
        for n, (src, dst) in enumerate(((z_hbm, z_in), *weights))
    ]
    for load in loads:
        load.start()

    barrier = pltpu.get_barrier_semaphore()
    for line in (y_peer, g_peer, z_peer):
        for step in range(1, GROUP):
            _, to_row, to_ch = line(step)
            pl.semaphore_signal(
                barrier, inc=1, device_id=(to_row, to_ch), device_id_type=MESH
            )
    loads[1].wait()
    wi_t[0] = flip(wi_in[0])
    loads[0].wait()
    zn = jnp.concatenate(
        [norm0(z_in[4 * a:4 * a + 4].reshape(128, 128).T).astype(BF16) for a in range(4)],
        axis=1,
    )
    for side in range(2):
        h_send[side] = glu(
            jnp.dot(wi_t[0, lanes(side, 256)], zn, preferred_element_type=F32)
        )
        if side == 0:
            pl.semaphore_wait(barrier, 3 * (GROUP - 1))
            for step in FAR_FIRST:
                _, to_row, to_ch = y_peer(step)
                pl.semaphore_signal(
                    ready, inc=1, device_id=(to_row, to_ch), device_id_type=MESH
                )
        spread(
            1, side, g_peer,
            lambda peer: h_send.at[side, pl.ds(pl.multiple_of(peer * 16, 16), 16), :],
            h_got.at[side, g],
        )
    pl.semaphore_wait(ready, GROUP - 1)

    for side in range(2):
        arrive(1, side, h_got.at[side])
        for a in range(4):
            for peer in range(GROUP):
                fan.at[a][pl.ds(peer, 16, stride=8), :] = h_got[
                    side, peer, :, lanes(a)
                ].astype(F32)
            rows = fan[a].reshape(4, 4, 8, 128)
            for b in range(4):
                i = 4 * a + b
                start, stride = (i // 2 * 16 + i % 2, 2) if side == 0 else (i, 16)
                mixed = jnp.concatenate(
                    [rows[:, t].reshape(32, 128)[:, lanes(b, 32)] for t in range(4)], axis=1
                )
                for q in range(4):
                    square.at[q][pl.ds(start, 8, stride=stride), :] = mixed[lanes(q, 8)]
        for q in range(4):
            k_send[4 * q:4 * q + 4, side] = square[q].T.reshape(4, 32, 128).astype(BF16)
        to_owners(
            2, side, lambda m: k_send.at[m, side],
            operands.at[
                0, side, pl.ds(pl.multiple_of(ch * 32, 32), 32),
                pl.ds(pl.multiple_of(zlo * 128, 128), 128),
            ],
        )

    z_send[...] = z_in[...].astype(BF16)
    spread(
        0, 0, y_peer,
        lambda peer: z_send.at[pl.ds(peer * 2, 2)],
        z_got.at[:, pl.ds(pl.multiple_of(y * 32, 32), 32), :],
    )
    for load in loads[2:]:
        load.wait()
    wi_t[1] = flip(wi_in[1])
    for u in range(2):
        wg_t[u] = flip(wg_in[u])
        wf_t[u] = flip(wf_in[u])

    @pl.when(is_owner)
    def _():
        arrive(2, 0, operands.at[0, 0])
        for q in range(4):
            turned[lanes(q), :] = operands[0, 0, :, lanes(q)].T
        arrive(2, 1, operands.at[0, 1])

        def back(step, carry):
            chunk = step // 4
            peer_zlo = (zlo + 1 + step) % 4
            rows = pl.ds(pl.multiple_of(peer_zlo * 128, 128), 128)
            columns = pl.ds(pl.multiple_of(chunk * 256, 256), 256)
            x1_send[chunk, rows, :] = jnp.dot(
                turned[rows, :], operands[0, 1, :, columns], preferred_element_type=F32
            ).astype(BF16)
            mine = c1_got.at[chunk, ch]

            def block(peer_ch):
                return x1_send.at[
                    chunk, pl.ds(place(peer_zlo, peer_ch // 2), 16),
                    pl.ds(pl.multiple_of(peer_ch % 2 * 128, 128), 128),
                ]

            for peer_ch in others():
                send(3, chunk, block(peer_ch), mine, plane(peer_zlo), peer_ch)

            @pl.when(peer_zlo == zlo)
            def _():
                keep(3, chunk, block(ch), mine)

            @pl.when(peer_zlo != zlo)
            def _():
                send(3, chunk, block(ch), mine, plane(peer_zlo), ch)

            return carry

        lax.fori_loop(0, 8, back, 0)

    arrive(0, 0, z_got)
    for chunk in range(2):
        for i in range(2):
            zt[chunk, :, lanes(i)] = jnp.concatenate(
                [z_got[i, lanes(part, 32), :].astype(F32) for part in range(chunk, 8, 2)],
                axis=0,
            ).T
        gate[chunk] = jax.nn.sigmoid(
            jnp.dot(wg_t[0], norm0(zt[chunk]).astype(BF16), preferred_element_type=F32)
        )

    def regroup(chunk):
        arrive(3, chunk, c1_got.at[chunk])
        swap(c1_got.at[chunk], lambda i: c2_send.at[chunk, i])
        spread(
            4, chunk, g_peer,
            lambda peer: c2_send.at[chunk, pl.ds(peer * 2, 2)],
            c2_got.at[chunk, :, pl.ds(pl.multiple_of(g * 16, 16), 16), :],
        )

    both(regroup)

    def middle(chunk):
        arrive(4, chunk, c2_got.at[chunk])
        product = jnp.concatenate(
            [c2_got[chunk, i].astype(F32) for i in range(2)], axis=1
        )
        acc[chunk] = gate[chunk] * jnp.dot(
            wf_t[0], norm0(product).astype(BF16), preferred_element_type=F32
        )
        normed = norm0(zt[chunk] + acc[chunk]).astype(BF16)
        for side in range(2):
            value = glu(
                jnp.dot(wi_t[1, lanes(side, 256)], normed, preferred_element_type=F32)
            )
            for i in range(2):
                b1_send[chunk, side, i] = value[:, lanes(i)]
        spread(
            5, chunk, g_peer,
            lambda peer: b1_send.at[
                chunk, :, :, pl.ds(pl.multiple_of(peer * 16, 16), 16), :
            ],
            b1_got.at[chunk, :, pl.ds(g * 2, 2)],
        )

    both(middle)

    def second_to_owners(chunk):
        arrive(5, chunk, b1_got.at[chunk])
        for side in range(2):
            swap(b1_got.at[chunk, side], lambda c: b2_send.at[chunk, c, side])
        to_owners(
            6, chunk, lambda m: b2_send.at[chunk, m],
            operands.at[
                1, :, pl.ds(place(zlo, y), 16),
                pl.ds(pl.multiple_of(chunk * 256 + zhi * 128, 128), 128),
            ],
        )

    both(second_to_owners)

    for chunk in range(2):
        for i in range(2):
            total = acc[chunk, :, lanes(i)].T.astype(BF16)
            for k in range(4):
                u_send[i, lanes(2 * k + chunk, 32), :] = total[lanes(k, 32)]
    spread(
        9, 0, y_peer,
        lambda peer: u_send.at[:, pl.ds(pl.multiple_of(peer * 32, 32), 32), :],
        u_got.at[pl.ds(y * 2, 2)],
    )

    @pl.when(is_owner)
    def _():
        for chunk in range(2):
            arrive(6, chunk, operands.at[1, :, :, pl.ds(chunk * 256, 256)])
            for q in (2 * chunk, 2 * chunk + 1):
                turned[lanes(q), :] = operands[1, 1, :, lanes(q)].T
        mine = t1_got.at[ch]
        own = y % 2 * 2 + zhi

        def back(step, carry):
            part = (own + 1 + step) % 4
            rows = pl.ds(pl.multiple_of(part * 128, 128), 128)
            x2_send[rows, :] = jnp.dot(
                turned[rows, :], operands[1, 0], preferred_element_type=F32
            ).astype(BF16)

            def go(peer_zlo, k, is_self=False):
                src = x2_send.at[
                    pl.ds(pl.multiple_of(part * 128 + k * 32, 32), 32),
                    pl.ds(pl.multiple_of(peer_zlo * 128, 128), 128),
                ]
                if is_self:
                    keep(7, 0, src, mine)
                else:
                    send(7, 0, src, mine, plane(peer_zlo),
                         (2 * k + part // 2) * 2 + part % 2)

            for dk in (2, 1, 3, 0):
                for dz in (2, 1, 3, 0):
                    if dk or dz:
                        go((zlo + dz) % 4, (y // 2 + dk) % 4)

            @pl.when(part == own)
            def _():
                go(zlo, y // 2, True)

            @pl.when(part != own)
            def _():
                go(zlo, y // 2)

            return carry

        lax.fori_loop(0, 4, back, 0)

    arrive(9, 0, u_got)
    for a in range(4):
        block = z_in[lanes(a, 4)] + u_got[lanes(a, 4)].astype(F32)
        middle_t[:, lanes(a)] = block.reshape(128, 128).T
    for half in range(2):
        normed = norm0(middle_t[:, lanes(half, 256)]).astype(BF16)
        home_gate[:, lanes(half, 256)] = jax.nn.sigmoid(
            jnp.dot(wg_t[1], normed, preferred_element_type=F32)
        )

    arrive(7, 0, t1_got)
    for q in range(4):
        square[q] = t1_got[lanes(q, 4)].astype(F32).reshape(128, 128).T
    for a in range(4):
        rows = [
            jnp.concatenate(
                [square.at[q][pl.ds(4 * a + b, 8, stride=16), :] for q in range(4)], axis=0
            )
            for b in range(4)
        ]
        for t in range(4):
            mixed = jnp.concatenate([rows[b][:, lanes(t, 32)] for b in range(4)], axis=1)
            for q in range(4):
                fan[a, lanes(4 * q + t, 8)] = mixed[lanes(q, 8)]
        for peer in range(GROUP):
            t2_send[a, peer] = fan.at[a][pl.ds(peer, 16, stride=8), :].astype(BF16)
        if a % 2:
            spread(
                8, a // 2, g_peer,
                lambda peer: t2_send.at[pl.ds(a - 1, 2), peer],
                t2_got.at[pl.ds(a - 1, 2), pl.ds(pl.multiple_of(g * 16, 16), 16), :],
            )
    for half in range(2):
        arrive(8, half, t2_got.at[pl.ds(2 * half, 2)])
        product = jnp.concatenate(
            [t2_got[2 * half + n].astype(F32) for n in range(2)], axis=1
        )
        there = lanes(half, 256)
        updated = middle_t[:, there] + home_gate[:, there] * jnp.dot(
            wf_t[1], norm0(product).astype(BF16), preferred_element_type=F32
        )
        for n in range(2):
            out_ref[lanes(2 * half + n, 4)] = updated[:, lanes(n)].T.reshape(4, 32, 128)

    leave(0, z_send.at[pl.ds(0, 14)])
    leave(1, h_send.at[:, pl.ds(0, 112), :])
    leave(4, c2_send.at[:, pl.ds(0, 14)])
    leave(5, b1_send.at[:, :, :, pl.ds(0, 112), :])
    leave(8, t2_send.at[:, pl.ds(0, 7)])
    leave(9, u_send.at[:, pl.ds(0, 224), :])

    @pl.when(is_owner)
    def _():
        leave(2, k_send.at[pl.ds(0, 15)])
        leave(3, size63)
        leave(6, b2_send.at[:, pl.ds(0, 15)])
        leave(7, size63)

    @pl.when(jnp.logical_not(is_owner))
    def _():
        leave(2, k_send)
        leave(6, b2_send)


def body(pair, out_inputs, out_gate, out_final, in_inputs, in_gate, in_final):
    anywhere = pl.BlockSpec(memory_space=pl.ANY)
    return pl.pallas_call(
        kernel,
        out_shape=jax.ShapeDtypeStruct((16, 32, 128), F32),
        in_specs=[anywhere] * 7,
        out_specs=pl.BlockSpec(memory_space=pltpu.VMEM),
        scratch_shapes=[
            pltpu.VMEM((16, 32, 128), F32),
            pltpu.VMEM((2, 128, 512), BF16),
            pltpu.VMEM((2, 128, 128), BF16),
            pltpu.VMEM((2, 128, 128), BF16),
            pltpu.VMEM((16, 32, 128), BF16),
            pltpu.VMEM((2, 256, 128), BF16),
            pltpu.VMEM((2, 512, 128), BF16),
            pltpu.VMEM((2, 128, 128), BF16),
            pltpu.VMEM((2, 128, 128), BF16),
            pltpu.VMEM((2, 128, 256), F32),
            pltpu.VMEM((2, 128, 256), F32),
            pltpu.VMEM((2, 128, 256), F32),
            pltpu.VMEM((2, 128, 512), BF16),
            pltpu.VMEM((2, 8, 16, 512), BF16),
            pltpu.VMEM((4, 128, 128), F32),
            pltpu.VMEM((4, 128, 128), F32),
            pltpu.VMEM((16, 2, 32, 128), BF16),
            pltpu.VMEM((2, 2, 2, 128, 128), BF16),
            pltpu.VMEM((2, 2, 16, 16, 128), BF16),
            pltpu.VMEM((256, 128), F32),
            pltpu.VMEM((2, 16, 2, 16, 128), BF16),
            pltpu.VMEM((2, 2, 512, 512), BF16),
            pltpu.VMEM((2, 512, 256), BF16),
            pltpu.VMEM((2, 16, 16, 128), BF16),
            pltpu.VMEM((2, 16, 16, 128), BF16),
            pltpu.VMEM((2, 2, 128, 128), BF16),
            pltpu.VMEM((512, 512), BF16),
            pltpu.VMEM((16, 32, 128), BF16),
            pltpu.VMEM((4, 8, 16, 128), BF16),
            pltpu.VMEM((4, 128, 128), BF16),
            pltpu.VMEM((2, 256, 128), BF16),
            pltpu.VMEM((16, 32, 128), BF16),
            pltpu.VMEM((128, 512), F32),
            pltpu.VMEM((128, 512), F32),
            pltpu.VMEM((512, 512), BF16),
            pltpu.VMEM((1008, 256), BF16),
            pltpu.SemaphoreType.DMA((PHASES,)),
            pltpu.SemaphoreType.DMA((PHASES, 2)),
            pltpu.SemaphoreType.DMA((7,)),
            pltpu.SemaphoreType.REGULAR,
        ],
        compiler_params=pltpu.CompilerParams(
            collective_id=0, has_side_effects=True, vmem_limit_bytes=60 * 1024 * 1024
        ),
        name="triangles",
    )(pair, out_inputs, out_gate, out_final, in_inputs, in_gate, in_final)


def solution(mesh):
    placed = (P("row", "ch", None), P(), P(), P(), P(), P(), P())
    return jax.shard_map(
        body, mesh=mesh, in_specs=placed, out_specs=P("row", "ch", None), check_vma=False
    )
```

```python
import jax
import jax.numpy as jnp
from jax import lax
from jax.experimental import pallas as pl
from jax.experimental.pallas import tpu as pltpu
from jax.sharding import PartitionSpec as P

MESH = pl.DeviceIdType.MESH
BF16 = jnp.bfloat16
F32 = jnp.float32
GROUP = 8
OWNERS = 16
FAR_FIRST = (4, 3, 5, 2, 6, 1, 7)
PHASES = 10


def mod(a, b):
    return lax.rem(a, jnp.int32(b))


def div(a, b):
    return lax.div(a, jnp.int32(b))


def norm0(values):
    mean = jnp.mean(values, axis=0, keepdims=True)
    centered = values - mean
    variance = jnp.mean(centered * centered, axis=0, keepdims=True)
    return centered * lax.rsqrt(variance + 1e-05)


def flip(w):
    return w.astype(F32).T.astype(BF16)


def place(zlo, y):
    return pl.multiple_of(zlo * 128 + y * 16, 16)


def kernel(
    z_hbm, wi0, wg0, wf0, wi1, wg1, wf1, out_hbm,
    z_in, wi_in, wg_in, wf_in, z_send, z_got, wi_t, wg_t, wf_t, zt, acc, gate,
    h_send, h_got, fan, square, k_send, b1_send, b1_got, turn, b2_send, operands,
    x1_send, c1_got, c2_send, c2_got, x2_send, t1_got, t2_send, t2_got,
    u_send, u_got, middle_t, home_gate, result, turned, size63, send_sem, recv_sem, in_sem, out_sem, ready,
):
    row = lax.axis_index("row")
    ch = lax.axis_index("ch")
    y, zhi = div(ch, 2), mod(ch, 2)
    x, zlo, core = div(row, 8), div(mod(row, 8), 2), mod(row, 2)
    g = x * 2 + core

    def owner_zlo(m):
        return mod(div(m, 2), 2) + 2 * mod(div(m, 4) + core, 2)

    def plane(peer_zlo):
        return x * 8 + peer_zlo * 2 + core

    is_owner = zlo == owner_zlo(ch)

    def send(phase, chunk, src, dst, to_row, to_ch):
        pltpu.make_async_remote_copy(
            src_ref=src, dst_ref=dst,
            send_sem=send_sem.at[phase], recv_sem=recv_sem.at[phase, chunk],
            device_id=(to_row, to_ch), device_id_type=MESH,
        ).start()

    def keep(phase, chunk, src, dst):
        pltpu.make_async_copy(src, dst, recv_sem.at[phase, chunk]).start()

    def arrive(phase, chunk, ref):
        pltpu.make_async_copy(ref, ref, recv_sem.at[phase, chunk]).wait()

    def leave(phase, ref):
        pltpu.make_async_copy(ref, ref, send_sem.at[phase]).wait()

    def y_peer(step):
        peer = mod(y + step, GROUP)
        return peer, row, peer * 2 + zhi

    def g_peer(step):
        peer = mod(g + step, GROUP)
        return peer, div(peer, 2) * 8 + zlo * 2 + mod(peer, 2), ch

    def z_peer(step):
        peer = mod(zhi * 4 + zlo + step, GROUP)
        return peer, plane(mod(peer, 4)), y * 2 + div(peer, 4)

    def spread(phase, chunk, peer_of, src_of, dst):
        for step in FAR_FIRST:
            peer, to_row, to_ch = peer_of(step)
            send(phase, chunk, src_of(peer), dst, to_row, to_ch)
        keep(phase, chunk, src_of(peer_of(0)[0]), dst)

    def others():
        for dy in (*FAR_FIRST, 0):
            for dz in (1, 0):
                if dy or dz:
                    yield mod(y + dy, 8) * 2 + mod(zhi + dz, 2)

    def to_owners(phase, chunk, src_of, here):
        for m in others():
            send(phase, chunk, src_of(m), here, plane(owner_zlo(m)), m)

        @pl.when(is_owner)
        def _():
            keep(phase, chunk, src_of(ch), here)

        @pl.when(jnp.logical_not(is_owner))
        def _():
            send(phase, chunk, src_of(ch), here, plane(owner_zlo(ch)), ch)

    def both(stage):
        def one(chunk, carry):
            stage(chunk)
            return carry

        lax.fori_loop(0, 2, one, 0)

    def swap(src, dst_of):
        turn[...] = src[...].astype(F32).reshape(256, 128)
        for b in range(16):
            dst_of(b)[...] = turn[pl.ds(b, 16, stride=16), :].astype(BF16)

    def lanes(n, width=128):
        return slice(n * width, (n + 1) * width)

    def glu(proj):
        return (jax.nn.sigmoid(proj[128:]) * proj[:128]).astype(BF16)

    weights = ((wi0, wi_in.at[0]), (wg0, wg_in.at[0]), (wf0, wf_in.at[0]),
               (wi1, wi_in.at[1]), (wg1, wg_in.at[1]), (wf1, wf_in.at[1]))
    loads = [
        pltpu.make_async_copy(src, dst, in_sem.at[n])
        for n, (src, dst) in enumerate(((z_hbm, z_in), *weights))
    ]
    for load in loads:
        load.start()

    barrier = pltpu.get_barrier_semaphore()
    for line in (y_peer, g_peer, z_peer):
        for step in range(1, GROUP):
            _, to_row, to_ch = line(step)
            pl.semaphore_signal(
                barrier, inc=1, device_id=(to_row, to_ch), device_id_type=MESH
            )
    loads[1].wait()
    wi_t[0] = flip(wi_in[0])
    loads[0].wait()
    zn = jnp.concatenate(
        [norm0(z_in[4 * a:4 * a + 4].reshape(128, 128).T).astype(BF16) for a in range(4)],
        axis=1,
    )
    for side in range(2):
        h_send[side] = glu(
            jnp.dot(wi_t[0, lanes(side, 256)], zn, preferred_element_type=F32)
        )
        if side == 0:
            pl.semaphore_wait(barrier, 3 * (GROUP - 1))
            for step in FAR_FIRST:
                _, to_row, to_ch = y_peer(step)
                pl.semaphore_signal(
                    ready, inc=1, device_id=(to_row, to_ch), device_id_type=MESH
                )
        spread(
            1, side, g_peer,
            lambda peer: h_send.at[side, pl.ds(pl.multiple_of(peer * 16, 16), 16), :],
            h_got.at[side, g],
        )
    pl.semaphore_wait(ready, GROUP - 1)

    for side in range(2):
        arrive(1, side, h_got.at[side])
        for a in range(4):
            for peer in range(GROUP):
                fan.at[a][pl.ds(peer, 16, stride=8), :] = h_got[
                    side, peer, :, lanes(a)
                ].astype(F32)
            rows = fan[a].reshape(4, 4, 8, 128)
            for b in range(4):
                i = 4 * a + b
                start, stride = (i // 2 * 16 + i % 2, 2) if side == 0 else (i, 16)
                mixed = jnp.concatenate(
                    [rows[:, t].reshape(32, 128)[:, lanes(b, 32)] for t in range(4)], axis=1
                )
                for q in range(4):
                    square.at[q][pl.ds(start, 8, stride=stride), :] = mixed[lanes(q, 8)]
        for q in range(4):
            k_send[4 * q:4 * q + 4, side] = square[q].T.reshape(4, 32, 128).astype(BF16)
        to_owners(
            2, side, lambda m: k_send.at[m, side],
            operands.at[
                0, side, pl.ds(pl.multiple_of(ch * 32, 32), 32),
                pl.ds(pl.multiple_of(zlo * 128, 128), 128),
            ],
        )

    z_send[...] = z_in[...].astype(BF16)
    spread(
        0, 0, y_peer,
        lambda peer: z_send.at[pl.ds(peer * 2, 2)],
        z_got.at[:, pl.ds(pl.multiple_of(y * 32, 32), 32), :],
    )
    for load in loads[2:]:
        load.wait()
    wi_t[1] = flip(wi_in[1])
    for u in range(2):
        wg_t[u] = flip(wg_in[u])
        wf_t[u] = flip(wf_in[u])

    @pl.when(is_owner)
    def _():
        arrive(2, 0, operands.at[0, 0])
        for q in range(4):
            turned[lanes(q), :] = operands[0, 0, :, lanes(q)].T
        arrive(2, 1, operands.at[0, 1])

        def back(step, carry):
            chunk = div(step, 4)
            peer_zlo = mod(zlo + 1 + step, 4)
            rows = pl.ds(pl.multiple_of(peer_zlo * 128, 128), 128)
            columns = pl.ds(pl.multiple_of(chunk * 256, 256), 256)
            x1_send[chunk, rows, :] = jnp.dot(
                turned[rows, :], operands[0, 1, :, columns], preferred_element_type=F32
            ).astype(BF16)
            mine = c1_got.at[chunk, ch]

            def block(peer_ch):
                return x1_send.at[
                    chunk, pl.ds(place(peer_zlo, div(peer_ch, 2)), 16),
                    pl.ds(pl.multiple_of(mod(peer_ch, 2) * 128, 128), 128),
                ]

            for peer_ch in others():
                send(3, chunk, block(peer_ch), mine, plane(peer_zlo), peer_ch)

            @pl.when(peer_zlo == zlo)
            def _():
                keep(3, chunk, block(ch), mine)

            @pl.when(peer_zlo != zlo)
            def _():
                send(3, chunk, block(ch), mine, plane(peer_zlo), ch)

            return carry

        lax.fori_loop(0, 8, back, 0)

    arrive(0, 0, z_got)
    for chunk in range(2):
        for i in range(2):
            zt[chunk, :, lanes(i)] = jnp.concatenate(
                [z_got[i, lanes(part, 32), :].astype(F32) for part in range(chunk, 8, 2)],
                axis=0,
            ).T
        gate[chunk] = jax.nn.sigmoid(
            jnp.dot(wg_t[0], norm0(zt[chunk]).astype(BF16), preferred_element_type=F32)
        )

    def regroup(chunk):
        arrive(3, chunk, c1_got.at[chunk])
        swap(c1_got.at[chunk], lambda i: c2_send.at[chunk, i])
        spread(
            4, chunk, g_peer,
            lambda peer: c2_send.at[chunk, pl.ds(peer * 2, 2)],
            c2_got.at[chunk, :, pl.ds(pl.multiple_of(g * 16, 16), 16), :],
        )

    both(regroup)

    def middle(chunk):
        arrive(4, chunk, c2_got.at[chunk])
        product = jnp.concatenate(
            [c2_got[chunk, i].astype(F32) for i in range(2)], axis=1
        )
        acc[chunk] = gate[chunk] * jnp.dot(
            wf_t[0], norm0(product).astype(BF16), preferred_element_type=F32
        )
        normed = norm0(zt[chunk] + acc[chunk]).astype(BF16)
        for side in range(2):
            value = glu(
                jnp.dot(wi_t[1, lanes(side, 256)], normed, preferred_element_type=F32)
            )
            for i in range(2):
                b1_send[chunk, side, i] = value[:, lanes(i)]
            spread(
                5, chunk * 2 + side, g_peer,
                lambda peer: b1_send.at[
                    chunk, side, :, pl.ds(pl.multiple_of(peer * 16, 16), 16), :
                ],
                b1_got.at[chunk, side, pl.ds(g * 2, 2)],
            )

    both(middle)

    def second_to_owners(chunk):
        for side in range(2):
            arrive(5, chunk * 2 + side, b1_got.at[chunk, side])
            swap(b1_got.at[chunk, side], lambda c: b2_send.at[chunk, side, c])
            to_owners(
                6, chunk, lambda m: b2_send.at[chunk, side, m],
                operands.at[
                    1, side, pl.ds(place(zlo, y), 16),
                    pl.ds(pl.multiple_of(chunk * 256 + zhi * 128, 128), 128),
                ],
            )

    both(second_to_owners)

    for chunk in range(2):
        for i in range(2):
            total = acc[chunk, :, lanes(i)].T.astype(BF16)
            for k in range(4):
                u_send[i, lanes(2 * k + chunk, 32), :] = total[lanes(k, 32)]
    spread(
        9, 0, y_peer,
        lambda peer: u_send.at[:, pl.ds(pl.multiple_of(peer * 32, 32), 32), :],
        u_got.at[pl.ds(y * 2, 2)],
    )

    @pl.when(is_owner)
    def _():
        for chunk in range(2):
            arrive(6, chunk, operands.at[1, :, :, pl.ds(chunk * 256, 256)])
            for q in (2 * chunk, 2 * chunk + 1):
                turned[lanes(q), :] = operands[1, 1, :, lanes(q)].T
        own = mod(y, 2) * 2 + zhi

        def back(step, carry):
            part, half = mod(own + 1 + step, 4), div(step, 4)
            rows = pl.ds(pl.multiple_of(part * 128, 128), 128)

            @pl.when(half == 0)
            def _():
                x2_send[rows, :] = jnp.dot(
                    turned[rows, :], operands[1, 0], preferred_element_type=F32
                ).astype(BF16)

            mine = t1_got.at[half, ch]

            def go(peer_zlo, k, is_self=False):
                src = x2_send.at[
                    pl.ds(pl.multiple_of(part * 128 + k * 32 + half * 16, 16), 16),
                    pl.ds(pl.multiple_of(peer_zlo * 128, 128), 128),
                ]
                if is_self:
                    keep(7, half, src, mine)
                else:
                    send(7, half, src, mine, plane(peer_zlo),
                         (2 * k + div(part, 2)) * 2 + mod(part, 2))

            for dk in (2, 1, 3, 0):
                for dz in (2, 1, 3, 0):
                    if dk or dz:
                        go(mod(zlo + dz, 4), mod(div(y, 2) + dk, 4))

            @pl.when(part == own)
            def _():
                go(zlo, div(y, 2), True)

            @pl.when(part != own)
            def _():
                go(zlo, div(y, 2))

            return carry

        lax.fori_loop(0, 8, back, 0)

    arrive(9, 0, u_got)
    for half in range(2):
        block = z_in[:, lanes(half, 16)] + u_got[:, lanes(half, 16)].astype(F32)
        middle_t[half] = block.reshape(256, 128).T
        home_gate[half] = jax.nn.sigmoid(
            jnp.dot(
                wg_t[1], norm0(middle_t[half]).astype(BF16), preferred_element_type=F32
            )
        )

    for half in range(2):
        arrive(7, half, t1_got.at[half])
        for q in range(2):
            square[q] = t1_got[half, lanes(q, 8)].astype(F32).reshape(128, 128).T
        for a in range(2):
            rows = [
                jnp.concatenate(
                    [square.at[q][pl.ds(8 * a + b, 8, stride=16), :] for q in range(2)],
                    axis=0,
                )
                for b in range(8)
            ]
            for t in range(8):
                mixed = jnp.concatenate([r[:, lanes(t, 16)] for r in rows], axis=1)
                for q in range(2):
                    fan[a, lanes(8 * q + t, 8)] = mixed[lanes(q, 8)]
            for peer in range(GROUP):
                t2_send[half, a, peer] = fan.at[a][pl.ds(peer, 16, stride=8), :].astype(BF16)
        spread(
            8, half, g_peer,
            lambda peer: t2_send.at[half, :, peer],
            t2_got.at[half, :, pl.ds(pl.multiple_of(g * 16, 16), 16), :],
        )
    stores = []
    for half in range(2):
        arrive(8, half, t2_got.at[half])
        product = jnp.concatenate([t2_got[half, a].astype(F32) for a in range(2)], axis=1)
        updated = middle_t[half] + home_gate[half] * jnp.dot(
            wf_t[1], norm0(product).astype(BF16), preferred_element_type=F32
        )
        there = pl.ds(half * 16, 16)
        result[:, there] = updated.T.reshape(16, 16, 128)
        store = pltpu.make_async_copy(
            result.at[:, there], out_hbm.at[:, there], out_sem.at[half]
        )
        store.start()
        stores.append(store)

    leave(0, z_send.at[pl.ds(0, 14)])
    leave(1, h_send.at[:, pl.ds(0, 112), :])
    leave(4, c2_send.at[:, pl.ds(0, 14)])
    leave(5, b1_send.at[:, :, :, pl.ds(0, 112), :])
    leave(8, t2_send.at[:, :, pl.ds(0, 7)])
    leave(9, u_send.at[:, pl.ds(0, 224), :])

    @pl.when(is_owner)
    def _():
        leave(2, k_send.at[pl.ds(0, 15)])
        leave(3, size63)
        leave(6, b2_send.at[:, :, pl.ds(0, 15)])
        leave(7, size63)

    @pl.when(jnp.logical_not(is_owner))
    def _():
        leave(2, k_send)
        leave(6, b2_send)

    for store in stores:
        store.wait()


def body(pair, out_inputs, out_gate, out_final, in_inputs, in_gate, in_final):
    anywhere = pl.BlockSpec(memory_space=pl.ANY)
    return pl.pallas_call(
        kernel,
        out_shape=jax.ShapeDtypeStruct((16, 32, 128), F32),
        in_specs=[anywhere] * 7,
        out_specs=anywhere,
        scratch_shapes=[
            pltpu.VMEM((16, 32, 128), F32),
            pltpu.VMEM((2, 128, 512), BF16),
            pltpu.VMEM((2, 128, 128), BF16),
            pltpu.VMEM((2, 128, 128), BF16),
            pltpu.VMEM((16, 32, 128), BF16),
            pltpu.VMEM((2, 256, 128), BF16),
            pltpu.VMEM((2, 512, 128), BF16),
            pltpu.VMEM((2, 128, 128), BF16),
            pltpu.VMEM((2, 128, 128), BF16),
            pltpu.VMEM((2, 128, 256), F32),
            pltpu.VMEM((2, 128, 256), F32),
            pltpu.VMEM((2, 128, 256), F32),
            pltpu.VMEM((2, 128, 512), BF16),
            pltpu.VMEM((2, 8, 16, 512), BF16),
            pltpu.VMEM((4, 128, 128), F32),
            pltpu.VMEM((4, 128, 128), F32),
            pltpu.VMEM((16, 2, 32, 128), BF16),
            pltpu.VMEM((2, 2, 2, 128, 128), BF16),
            pltpu.VMEM((2, 2, 16, 16, 128), BF16),
            pltpu.VMEM((256, 128), F32),
            pltpu.VMEM((2, 2, 16, 16, 128), BF16),
            pltpu.VMEM((2, 2, 512, 512), BF16),
            pltpu.VMEM((2, 512, 256), BF16),
            pltpu.VMEM((2, 16, 16, 128), BF16),
            pltpu.VMEM((2, 16, 16, 128), BF16),
            pltpu.VMEM((2, 2, 128, 128), BF16),
            pltpu.VMEM((512, 512), BF16),
            pltpu.VMEM((2, 16, 16, 128), BF16),
            pltpu.VMEM((2, 2, 8, 16, 128), BF16),
            pltpu.VMEM((2, 2, 128, 128), BF16),
            pltpu.VMEM((2, 256, 128), BF16),
            pltpu.VMEM((16, 32, 128), BF16),
            pltpu.VMEM((2, 128, 256), F32),
            pltpu.VMEM((2, 128, 256), F32),
            pltpu.VMEM((16, 32, 128), F32),
            pltpu.VMEM((512, 512), BF16),
            pltpu.VMEM((1008, 256), BF16),
            pltpu.SemaphoreType.DMA((PHASES,)),
            pltpu.SemaphoreType.DMA((PHASES, 4)),
            pltpu.SemaphoreType.DMA((7,)),
            pltpu.SemaphoreType.DMA((2,)),
            pltpu.SemaphoreType.REGULAR,
        ],
        compiler_params=pltpu.CompilerParams(
            collective_id=0, has_side_effects=True, vmem_limit_bytes=60 * 1024 * 1024
        ),
        name="triangles",
    )(pair, out_inputs, out_gate, out_final, in_inputs, in_gate, in_final)


def solution(mesh):
    placed = (P("row", "ch", None), P(), P(), P(), P(), P(), P())
    return jax.shard_map(
        body, mesh=mesh, in_specs=placed, out_specs=P("row", "ch", None), check_vma=False
    )
```

```python
import jax
import jax.numpy as jnp
from jax import lax
from jax.experimental import pallas as pl
from jax.experimental.pallas import tpu as pltpu
from jax.sharding import PartitionSpec as P

MESH = pl.DeviceIdType.MESH
BF16 = jnp.bfloat16
F32 = jnp.float32
GROUP = 8
OWNERS = 16
FAR_FIRST = (4, 3, 5, 2, 6, 1, 7)
PHASES = 12


def mod(a, b):
    return lax.rem(a, jnp.int32(b))


def div(a, b):
    return lax.div(a, jnp.int32(b))


def norm0(values):
    mean = jnp.mean(values, axis=0, keepdims=True)
    centered = values - mean
    variance = jnp.mean(centered * centered, axis=0, keepdims=True)
    return centered * lax.rsqrt(variance + 1e-05)


def flip(w):
    return w.astype(F32).T.astype(BF16)


def place(zlo, y):
    return pl.multiple_of(zlo * 128 + y * 16, 16)


def kernel(
    z_hbm, wi0, wg0, wf0, wi1, wg1, wf1, out_hbm,
    z_in, wi_in, wg_in, wf_in, z_send, z_got, wi_t, wg_t, wf_t, zt, acc, gate,
    h_send, h_got, fan, square, k_send, b1_send, b1_got, turn, b2_send, operands,
    x1_send, c1_got, c2_send, c2_got, x2_send, t1_got, t2_send, t2_got,
    u_send, u_got, middle_t, home_gate, result, turned, size63, send_sem, recv_sem, in_sem, out_sem, ready,
):
    row = lax.axis_index("row")
    ch = lax.axis_index("ch")
    y, zhi = div(ch, 2), mod(ch, 2)
    x, zlo, core = div(row, 8), div(mod(row, 8), 2), mod(row, 2)
    g = x * 2 + core

    def owner_zlo(m, of_core=core):
        return mod(div(m, 2), 2) + 2 * mod(div(m, 4) + of_core, 2)

    def plane(peer_zlo, of_core=core):
        return x * 8 + peer_zlo * 2 + of_core

    other_core = 1 - core
    is_owner = zlo == owner_zlo(ch)
    is_mate = zlo == owner_zlo(ch, other_core)

    def send(phase, chunk, src, dst, to_row, to_ch):
        pltpu.make_async_remote_copy(
            src_ref=src, dst_ref=dst,
            send_sem=send_sem.at[phase], recv_sem=recv_sem.at[phase, chunk],
            device_id=(to_row, to_ch), device_id_type=MESH,
        ).start()

    def keep(phase, chunk, src, dst):
        pltpu.make_async_copy(src, dst, recv_sem.at[phase, chunk]).start()

    def arrive(phase, chunk, ref):
        pltpu.make_async_copy(ref, ref, recv_sem.at[phase, chunk]).wait()

    def leave(phase, ref):
        pltpu.make_async_copy(ref, ref, send_sem.at[phase]).wait()

    def y_peer(step):
        peer = mod(y + step, GROUP)
        return peer, row, peer * 2 + zhi

    def g_peer(step):
        peer = mod(g + step, GROUP)
        return peer, div(peer, 2) * 8 + zlo * 2 + mod(peer, 2), ch

    def z_peer(step):
        peer = mod(zhi * 4 + zlo + step, GROUP)
        return peer, plane(mod(peer, 4)), y * 2 + div(peer, 4)

    def spread(phase, chunk, peer_of, src_of, dst):
        for step in FAR_FIRST:
            peer, to_row, to_ch = peer_of(step)
            send(phase, chunk, src_of(peer), dst, to_row, to_ch)
        keep(phase, chunk, src_of(peer_of(0)[0]), dst)

    def others():
        for dy in (*FAR_FIRST, 0):
            for dz in (1, 0):
                if dy or dz:
                    yield mod(y + dy, 8) * 2 + mod(zhi + dz, 2)

    def to_owners(phase, chunk, src_of, here):
        for m in others():
            send(phase, chunk, src_of(m), here, plane(owner_zlo(m)), m)

        @pl.when(is_owner)
        def _():
            keep(phase, chunk, src_of(ch), here)

        @pl.when(jnp.logical_not(is_owner))
        def _():
            send(phase, chunk, src_of(ch), here, plane(owner_zlo(ch)), ch)

    def both(stage):
        def one(chunk, carry):
            stage(chunk)
            return carry

        lax.fori_loop(0, 2, one, 0)

    def swap(src, dst_of):
        turn[...] = src[...].astype(F32).reshape(256, 128)
        for b in range(16):
            dst_of(b)[...] = turn[pl.ds(b, 16, stride=16), :].astype(BF16)

    def lanes(n, width=128):
        return slice(n * width, (n + 1) * width)

    def glu(proj):
        return (jax.nn.sigmoid(proj[128:]) * proj[:128]).astype(BF16)

    weights = ((wi0, wi_in.at[0]), (wg0, wg_in.at[0]), (wf0, wf_in.at[0]),
               (wi1, wi_in.at[1]), (wg1, wg_in.at[1]), (wf1, wf_in.at[1]))
    loads = [
        pltpu.make_async_copy(src, dst, in_sem.at[n])
        for n, (src, dst) in enumerate(((z_hbm, z_in), *weights))
    ]
    for load in loads:
        load.start()

    barrier = pltpu.get_barrier_semaphore()
    for line in (y_peer, g_peer, z_peer):
        for step in range(1, GROUP):
            _, to_row, to_ch = line(step)
            pl.semaphore_signal(
                barrier, inc=1, device_id=(to_row, to_ch), device_id_type=MESH
            )
    loads[1].wait()
    wi_t[0] = flip(wi_in[0])
    loads[0].wait()
    zn = jnp.concatenate(
        [norm0(z_in[4 * a:4 * a + 4].reshape(128, 128).T).astype(BF16) for a in range(4)],
        axis=1,
    )
    for side in range(2):
        h_send[side] = glu(
            jnp.dot(wi_t[0, lanes(side, 256)], zn, preferred_element_type=F32)
        )
        if side == 0:
            pl.semaphore_wait(barrier, 3 * (GROUP - 1))
            for step in FAR_FIRST:
                _, to_row, to_ch = y_peer(step)
                pl.semaphore_signal(
                    ready, inc=1, device_id=(to_row, to_ch), device_id_type=MESH
                )
        spread(
            1, side, g_peer,
            lambda peer: h_send.at[side, pl.ds(pl.multiple_of(peer * 16, 16), 16), :],
            h_got.at[side, g],
        )
    pl.semaphore_wait(ready, GROUP - 1)

    for side in range(2):
        arrive(1, side, h_got.at[side])
        for a in range(4):
            for peer in range(GROUP):
                fan.at[a][pl.ds(peer, 16, stride=8), :] = h_got[
                    side, peer, :, lanes(a)
                ].astype(F32)
            rows = fan[a].reshape(4, 4, 8, 128)
            for b in range(4):
                i = 4 * a + b
                start, stride = (i // 2 * 16 + i % 2, 2) if side == 0 else (i, 16)
                mixed = jnp.concatenate(
                    [rows[:, t].reshape(32, 128)[:, lanes(b, 32)] for t in range(4)], axis=1
                )
                for q in range(4):
                    square.at[q][pl.ds(start, 8, stride=stride), :] = mixed[lanes(q, 8)]
        for q in range(4):
            k_send[4 * q:4 * q + 4, side] = square[q].T.reshape(4, 32, 128).astype(BF16)
        to_owners(
            2, side, lambda m: k_send.at[m, side],
            operands.at[
                0, side, pl.ds(pl.multiple_of(ch * 32, 32), 32),
                pl.ds(pl.multiple_of(zlo * 128, 128), 128),
            ],
        )

    z_send[...] = z_in[...].astype(BF16)
    spread(
        0, 0, y_peer,
        lambda peer: z_send.at[pl.ds(peer * 2, 2)],
        z_got.at[:, pl.ds(pl.multiple_of(y * 32, 32), 32), :],
    )
    for load in loads[2:]:
        load.wait()
    wi_t[1] = flip(wi_in[1])
    for u in range(2):
        wg_t[u] = flip(wg_in[u])
        wf_t[u] = flip(wf_in[u])

    def part_of(step):
        peer_zlo = mod(zlo + 1 + step, 4)
        return peer_zlo, pl.ds(pl.multiple_of(peer_zlo * 128, 128), 128)

    def block(chunk, peer_zlo, peer_ch):
        return x1_send.at[
            chunk, pl.ds(place(peer_zlo, div(peer_ch, 2)), 16),
            pl.ds(pl.multiple_of(mod(peer_ch, 2) * 128, 128), 128),
        ]

    @pl.when(is_owner)
    def _():
        arrive(2, 0, operands.at[0, 0])
        for q in range(4):
            turned[lanes(q), :] = operands[0, 0, :, lanes(q)].T
        arrive(2, 1, operands.at[0, 1])

        mine = c1_got.at[0, ch]

        def back(step, carry):
            peer_zlo, rows = part_of(step)
            product = jnp.dot(
                turned[rows, :], operands[0, 1], preferred_element_type=F32
            ).astype(BF16)
            x1_send[1, rows, :] = product[:, 256:]
            there = x1_send.at[1, rows, :]
            send(10, step, there, there, plane(zlo, other_core), ch)
            x1_send[0, rows, :] = product[:, :256]
            for peer_ch in others():
                send(3, 0, block(0, peer_zlo, peer_ch), mine, plane(peer_zlo), peer_ch)

            @pl.when(peer_zlo == zlo)
            def _():
                keep(3, 0, block(0, peer_zlo, ch), mine)

            @pl.when(peer_zlo != zlo)
            def _():
                send(3, 0, block(0, peer_zlo, ch), mine, plane(peer_zlo), ch)

            return carry

        lax.fori_loop(0, 4, back, 0)

    @pl.when(is_mate)
    def _():
        def back(step, carry):
            peer_zlo, rows = part_of(step)
            arrive(10, step, x1_send.at[1, rows, :])
            for peer_ch in (*others(), ch):
                send(3, 1, block(1, peer_zlo, peer_ch), c1_got.at[1, ch],
                     plane(peer_zlo, other_core), peer_ch)
            return carry

        lax.fori_loop(0, 4, back, 0)

    arrive(0, 0, z_got)
    for chunk in range(2):
        for i in range(2):
            zt[chunk, :, lanes(i)] = jnp.concatenate(
                [z_got[i, lanes(part, 32), :].astype(F32) for part in range(chunk, 8, 2)],
                axis=0,
            ).T
        gate[chunk] = jax.nn.sigmoid(
            jnp.dot(wg_t[0], norm0(zt[chunk]).astype(BF16), preferred_element_type=F32)
        )

    def regroup(chunk):
        arrive(3, chunk, c1_got.at[chunk])
        swap(c1_got.at[chunk], lambda i: c2_send.at[chunk, i])
        spread(
            4, chunk, g_peer,
            lambda peer: c2_send.at[chunk, pl.ds(peer * 2, 2)],
            c2_got.at[chunk, :, pl.ds(pl.multiple_of(g * 16, 16), 16), :],
        )

    both(regroup)

    def middle(chunk):
        arrive(4, chunk, c2_got.at[chunk])
        product = jnp.concatenate(
            [c2_got[chunk, i].astype(F32) for i in range(2)], axis=1
        )
        acc[chunk] = gate[chunk] * jnp.dot(
            wf_t[0], norm0(product).astype(BF16), preferred_element_type=F32
        )
        normed = norm0(zt[chunk] + acc[chunk]).astype(BF16)
        for side in range(2):
            value = glu(
                jnp.dot(wi_t[1, lanes(side, 256)], normed, preferred_element_type=F32)
            )
            for i in range(2):
                b1_send[chunk, side, i] = value[:, lanes(i)]
        spread(
            5, chunk, g_peer,
            lambda peer: b1_send.at[
                chunk, :, :, pl.ds(pl.multiple_of(peer * 16, 16), 16), :
            ],
            b1_got.at[chunk, :, pl.ds(g * 2, 2)],
        )

    both(middle)

    def second_to_owners(chunk):
        arrive(5, chunk, b1_got.at[chunk])
        for side in range(2):
            swap(b1_got.at[chunk, side], lambda c: b2_send.at[chunk, c, side])
        to_owners(
            6, chunk, lambda m: b2_send.at[chunk, m],
            operands.at[
                1, :, pl.ds(place(zlo, y), 16),
                pl.ds(pl.multiple_of(chunk * 256 + zhi * 128, 128), 128),
            ],
        )

    both(second_to_owners)

    for chunk in range(2):
        for i in range(2):
            total = acc[chunk, :, lanes(i)].T.astype(BF16)
            for k in range(4):
                u_send[i, lanes(2 * k + chunk, 32), :] = total[lanes(k, 32)]
    spread(
        9, 0, y_peer,
        lambda peer: u_send.at[:, pl.ds(pl.multiple_of(peer * 32, 32), 32), :],
        u_got.at[pl.ds(y * 2, 2)],
    )

    own = mod(y, 2) * 2 + zhi

    def columns_part(step):
        part = mod(own + 1 + step, 4)
        return part, pl.ds(pl.multiple_of(part * 128, 128), 128)

    def piece(part, peer_zlo, k):
        return x2_send.at[
            pl.ds(pl.multiple_of(part * 128 + k * 32, 32), 32),
            pl.ds(pl.multiple_of(peer_zlo * 128, 128), 128),
        ]

    def go(part, of_core, with_self=True):
        for dk in (2, 1, 3, 0):
            for dz in (2, 1, 3, 0):
                if dk or dz or with_self:
                    peer_zlo, k = mod(zlo + dz, 4), mod(div(y, 2) + dk, 4)
                    send(7, 0, piece(part, peer_zlo, k), t1_got.at[ch],
                         plane(peer_zlo, of_core), (2 * k + div(part, 2)) * 2 + mod(part, 2))

    @pl.when(is_owner)
    def _():
        for chunk in range(2):
            arrive(6, chunk, operands.at[1, :, :, pl.ds(chunk * 256, 256)])
            for q in (2 * chunk, 2 * chunk + 1):
                turned[lanes(q), :] = operands[1, 1, :, lanes(q)].T

        def multiply(rows):
            x2_send[rows, :] = jnp.dot(
                turned[rows, :], operands[1, 0], preferred_element_type=F32
            ).astype(BF16)

        for step in range(0, 4, 2):
            part, rows = columns_part(step)
            multiply(rows)
            there = x2_send.at[rows, :]
            send(11, step, there, there, plane(zlo, other_core), ch)
            part, rows = columns_part(step + 1)
            multiply(rows)
            go(part, core, with_self=step == 0)
        keep(7, 0, piece(own, zlo, div(y, 2)), t1_got.at[ch])

    @pl.when(is_mate)
    def _():
        for step in range(0, 4, 2):
            part, rows = columns_part(step)
            arrive(11, step, x2_send.at[rows, :])
            go(part, other_core)

    arrive(9, 0, u_got)
    for a in range(4):
        block = z_in[lanes(a, 4)] + u_got[lanes(a, 4)].astype(F32)
        middle_t[:, lanes(a)] = block.reshape(128, 128).T
    for half in range(2):
        normed = norm0(middle_t[:, lanes(half, 256)]).astype(BF16)
        home_gate[:, lanes(half, 256)] = jax.nn.sigmoid(
            jnp.dot(wg_t[1], normed, preferred_element_type=F32)
        )

    arrive(7, 0, t1_got)
    for q in range(4):
        square[q] = t1_got[lanes(q, 4)].astype(F32).reshape(128, 128).T
    for a in range(4):
        rows = [
            jnp.concatenate(
                [square.at[q][pl.ds(4 * a + b, 8, stride=16), :] for q in range(4)], axis=0
            )
            for b in range(4)
        ]
        for t in range(4):
            mixed = jnp.concatenate([rows[b][:, lanes(t, 32)] for b in range(4)], axis=1)
            for q in range(4):
                fan[a, lanes(4 * q + t, 8)] = mixed[lanes(q, 8)]
        for peer in range(GROUP):
            t2_send[a, peer] = fan.at[a][pl.ds(peer, 16, stride=8), :].astype(BF16)
        if a % 2:
            spread(
                8, a // 2, g_peer,
                lambda peer: t2_send.at[pl.ds(a - 1, 2), peer],
                t2_got.at[pl.ds(a - 1, 2), pl.ds(pl.multiple_of(g * 16, 16), 16), :],
            )
    stores = []
    for half in range(2):
        arrive(8, half, t2_got.at[pl.ds(2 * half, 2)])
        product = jnp.concatenate(
            [t2_got[2 * half + n].astype(F32) for n in range(2)], axis=1
        )
        there = lanes(half, 256)
        updated = middle_t[:, there] + home_gate[:, there] * jnp.dot(
            wf_t[1], norm0(product).astype(BF16), preferred_element_type=F32
        )
        home = pl.ds(half * 8, 8)
        result[home] = updated.T.reshape(8, 32, 128)
        store = pltpu.make_async_copy(result.at[home], out_hbm.at[home], out_sem.at[half])
        store.start()
        stores.append(store)

    leave(0, z_send.at[pl.ds(0, 14)])
    leave(1, h_send.at[:, pl.ds(0, 112), :])
    leave(4, c2_send.at[:, pl.ds(0, 14)])
    leave(5, b1_send.at[:, :, :, pl.ds(0, 112), :])
    leave(8, t2_send.at[:, pl.ds(0, 7)])
    leave(9, u_send.at[:, pl.ds(0, 224), :])

    @pl.when(is_owner)
    def _():
        leave(2, k_send.at[pl.ds(0, 15)])
        leave(3, size63)
        leave(6, b2_send.at[:, pl.ds(0, 15)])
        leave(7, size63.at[pl.ds(0, 992)])
        leave(10, x1_send.at[1])
        leave(11, x2_send.at[pl.ds(0, 256)])

    @pl.when(jnp.logical_not(is_owner))
    def _():
        leave(2, k_send)
        leave(6, b2_send)

    @pl.when(is_mate)
    def _():
        leave(3, x1_send.at[1])
        leave(7, x2_send.at[pl.ds(0, 256)])

    for store in stores:
        store.wait()


def body(pair, out_inputs, out_gate, out_final, in_inputs, in_gate, in_final):
    anywhere = pl.BlockSpec(memory_space=pl.ANY)
    return pl.pallas_call(
        kernel,
        out_shape=jax.ShapeDtypeStruct((16, 32, 128), F32),
        in_specs=[anywhere] * 7,
        out_specs=anywhere,
        scratch_shapes=[
            pltpu.VMEM((16, 32, 128), F32),
            pltpu.VMEM((2, 128, 512), BF16),
            pltpu.VMEM((2, 128, 128), BF16),
            pltpu.VMEM((2, 128, 128), BF16),
            pltpu.VMEM((16, 32, 128), BF16),
            pltpu.VMEM((2, 256, 128), BF16),
            pltpu.VMEM((2, 512, 128), BF16),
            pltpu.VMEM((2, 128, 128), BF16),
            pltpu.VMEM((2, 128, 128), BF16),
            pltpu.VMEM((2, 128, 256), F32),
            pltpu.VMEM((2, 128, 256), F32),
            pltpu.VMEM((2, 128, 256), F32),
            pltpu.VMEM((2, 128, 512), BF16),
            pltpu.VMEM((2, 8, 16, 512), BF16),
            pltpu.VMEM((4, 128, 128), F32),
            pltpu.VMEM((4, 128, 128), F32),
            pltpu.VMEM((16, 2, 32, 128), BF16),
            pltpu.VMEM((2, 2, 2, 128, 128), BF16),
            pltpu.VMEM((2, 2, 16, 16, 128), BF16),
            pltpu.VMEM((256, 128), F32),
            pltpu.VMEM((2, 16, 2, 16, 128), BF16),
            pltpu.VMEM((2, 2, 512, 512), BF16),
            pltpu.VMEM((2, 512, 256), BF16),
            pltpu.VMEM((2, 16, 16, 128), BF16),
            pltpu.VMEM((2, 16, 16, 128), BF16),
            pltpu.VMEM((2, 2, 128, 128), BF16),
            pltpu.VMEM((512, 512), BF16),
            pltpu.VMEM((16, 32, 128), BF16),
            pltpu.VMEM((4, 8, 16, 128), BF16),
            pltpu.VMEM((4, 128, 128), BF16),
            pltpu.VMEM((2, 256, 128), BF16),
            pltpu.VMEM((16, 32, 128), BF16),
            pltpu.VMEM((128, 512), F32),
            pltpu.VMEM((128, 512), F32),
            pltpu.VMEM((16, 32, 128), F32),
            pltpu.VMEM((512, 512), BF16),
            pltpu.VMEM((1008, 128), BF16),
            pltpu.SemaphoreType.DMA((PHASES,)),
            pltpu.SemaphoreType.DMA((PHASES, 4)),
            pltpu.SemaphoreType.DMA((7,)),
            pltpu.SemaphoreType.DMA((2,)),
            pltpu.SemaphoreType.REGULAR,
        ],
        compiler_params=pltpu.CompilerParams(
            collective_id=0, has_side_effects=True, vmem_limit_bytes=60 * 1024 * 1024
        ),
        name="triangles",
    )(pair, out_inputs, out_gate, out_final, in_inputs, in_gate, in_final)


def solution(mesh):
    placed = (P("row", "ch", None), P(), P(), P(), P(), P(), P())
    return jax.shard_map(
        body, mesh=mesh, in_specs=placed, out_specs=P("row", "ch", None), check_vma=False
    )
```

```python
import jax
import jax.numpy as jnp
from jax import lax
from jax.experimental import pallas as pl
from jax.experimental.pallas import tpu as pltpu
from jax.sharding import PartitionSpec as P

MESH = pl.DeviceIdType.MESH
BF16 = jnp.bfloat16
F32 = jnp.float32
GROUP = 8
OWNERS = 16
FAR_FIRST = (4, 3, 5, 2, 6, 1, 7)
PHASES = 10


def norm0(values):
    mean = jnp.mean(values, axis=0, keepdims=True)
    centered = values - mean
    variance = jnp.mean(centered * centered, axis=0, keepdims=True)
    return centered * lax.rsqrt(variance + 1e-05)


def flip(w):
    return w.astype(F32).T.astype(BF16)


def place(zlo, y):
    return pl.multiple_of(zlo * 128 + y * 16, 16)


def kernel(
    z_hbm, wi0, wg0, wf0, wi1, wg1, wf1, out_ref,
    z_in, wi_in, wg_in, wf_in, z_send, z_got, wi_t, wg_t, wf_t, zt, acc, gate,
    h_send, h_got, fan, square, k_send, b1_send, b1_got, turn, b2_send, operands,
    x1_send, c1_got, c2_send, c2_got, x2_send, t1_got, t2_send, t2_got,
    u_send, u_got, middle_t, home_gate, turned, size63, send_sem, recv_sem, in_sem, ready,
):
    row = lax.axis_index("row")
    ch = lax.axis_index("ch")
    y, zhi = ch // 2, ch % 2
    x, zlo, core = row // 8, row % 8 // 2, row % 2
    g = x * 2 + core

    def owner_zlo(m):
        return m // 2 % 2 + 2 * ((m // 4 + core) % 2)

    def plane(peer_zlo):
        return x * 8 + peer_zlo * 2 + core

    is_owner = zlo == owner_zlo(ch)

    def send(phase, chunk, src, dst, to_row, to_ch):
        pltpu.make_async_remote_copy(
            src_ref=src, dst_ref=dst,
            send_sem=send_sem.at[phase], recv_sem=recv_sem.at[phase, chunk],
            device_id=(to_row, to_ch), device_id_type=MESH,
        ).start()

    def keep(phase, chunk, src, dst):
        pltpu.make_async_copy(src, dst, recv_sem.at[phase, chunk]).start()

    def arrive(phase, chunk, ref):
        pltpu.make_async_copy(ref, ref, recv_sem.at[phase, chunk]).wait()

    def leave(phase, ref):
        pltpu.make_async_copy(ref, ref, send_sem.at[phase]).wait()

    def y_peer(step):
        peer = (y + step) % GROUP
        return peer, row, peer * 2 + zhi

    def g_peer(step):
        peer = (g + step) % GROUP
        return peer, peer // 2 * 8 + zlo * 2 + peer % 2, ch

    def z_peer(step):
        peer = (zhi * 4 + zlo + step) % GROUP
        return peer, plane(peer % 4), y * 2 + peer // 4

    def spread(phase, chunk, peer_of, src_of, dst):
        for step in FAR_FIRST:
            peer, to_row, to_ch = peer_of(step)
            send(phase, chunk, src_of(peer), dst, to_row, to_ch)
        keep(phase, chunk, src_of(peer_of(0)[0]), dst)

    def others():
        for dy in (*FAR_FIRST, 0):
            for dz in (1, 0):
                if dy or dz:
                    yield (y + dy) % 8 * 2 + (zhi + dz) % 2

    def to_owners(phase, chunk, src_of, here):
        for m in others():
            send(phase, chunk, src_of(m), here, plane(owner_zlo(m)), m)

        @pl.when(is_owner)
        def _():
            keep(phase, chunk, src_of(ch), here)

        @pl.when(jnp.logical_not(is_owner))
        def _():
            send(phase, chunk, src_of(ch), here, plane(owner_zlo(ch)), ch)

    def both(stage):
        def one(chunk, carry):
            stage(chunk)
            return carry

        lax.fori_loop(0, 2, one, 0)

    def swap(src, dst_of):
        turn[...] = src[...].astype(F32).reshape(256, 128)
        for b in range(16):
            dst_of(b)[...] = turn[pl.ds(b, 16, stride=16), :].astype(BF16)

    def lanes(n, width=128):
        return slice(n * width, (n + 1) * width)

    def glu(proj):
        return (jax.nn.sigmoid(proj[128:]) * proj[:128]).astype(BF16)

    weights = ((wi0, wi_in.at[0]), (wg0, wg_in.at[0]), (wf0, wf_in.at[0]),
               (wi1, wi_in.at[1]), (wg1, wg_in.at[1]), (wf1, wf_in.at[1]))
    loads = [
        pltpu.make_async_copy(src, dst, in_sem.at[n])
        for n, (src, dst) in enumerate(((z_hbm, z_in), *weights))
    ]
    for load in loads:
        load.start()

    barrier = pltpu.get_barrier_semaphore()
    for line in (y_peer, g_peer, z_peer):
        for step in range(1, GROUP):
            _, to_row, to_ch = line(step)
            pl.semaphore_signal(
                barrier, inc=1, device_id=(to_row, to_ch), device_id_type=MESH
            )
    loads[1].wait()
    wi_t[0] = flip(wi_in[0])
    loads[0].wait()
    zn = jnp.concatenate(
        [norm0(z_in[4 * a:4 * a + 4].reshape(128, 128).T).astype(BF16) for a in range(4)],
        axis=1,
    )
    for side in range(2):
        h_send[side] = glu(
            jnp.dot(wi_t[0, lanes(side, 256)], zn, preferred_element_type=F32)
        )
        if side == 0:
            pl.semaphore_wait(barrier, 3 * (GROUP - 1))
            for step in FAR_FIRST:
                _, to_row, to_ch = y_peer(step)
                pl.semaphore_signal(
                    ready, inc=1, device_id=(to_row, to_ch), device_id_type=MESH
                )
        spread(
            1, side, g_peer,
            lambda peer: h_send.at[side, pl.ds(pl.multiple_of(peer * 16, 16), 16), :],
            h_got.at[side, g],
        )
    pl.semaphore_wait(ready, GROUP - 1)

    for side in range(2):
        arrive(1, side, h_got.at[side])
        for a in range(4):
            for peer in range(GROUP):
                fan.at[a][pl.ds(peer, 16, stride=8), :] = h_got[
                    side, peer, :, lanes(a)
                ].astype(F32)
            rows = fan[a].reshape(4, 4, 8, 128)
            for b in range(4):
                i = 4 * a + b
                start, stride = (i // 2 * 16 + i % 2, 2) if side == 0 else (i, 16)
                mixed = jnp.concatenate(
                    [rows[:, t].reshape(32, 128)[:, lanes(b, 32)] for t in range(4)], axis=1
                )
                for q in range(4):
                    square.at[q][pl.ds(start, 8, stride=stride), :] = mixed[lanes(q, 8)]
        for q in range(4):
            k_send[4 * q:4 * q + 4, side] = square[q].T.reshape(4, 32, 128).astype(BF16)
        to_owners(
            2, side, lambda m: k_send.at[m, side],
            operands.at[
                0, side, pl.ds(pl.multiple_of(ch * 32, 32), 32),
                pl.ds(pl.multiple_of(zlo * 128, 128), 128),
            ],
        )

    z_send[...] = z_in[...].astype(BF16)
    spread(
        0, 0, y_peer,
        lambda peer: z_send.at[pl.ds(peer * 2, 2)],
        z_got.at[:, pl.ds(pl.multiple_of(y * 32, 32), 32), :],
    )
    for load in loads[2:]:
        load.wait()
    wi_t[1] = flip(wi_in[1])
    for u in range(2):
        wg_t[u] = flip(wg_in[u])
        wf_t[u] = flip(wf_in[u])

    @pl.when(is_owner)
    def _():
        arrive(2, 0, operands.at[0, 0])
        for q in range(4):
            turned[lanes(q), :] = operands[0, 0, :, lanes(q)].T
        arrive(2, 1, operands.at[0, 1])

        mine = c1_got.at[:, ch]

        def back(step, carry):
            peer_zlo = (zlo + 1 + step) % 4
            rows = pl.ds(pl.multiple_of(peer_zlo * 128, 128), 128)
            product = jnp.dot(
                turned[rows, :], operands[0, 1], preferred_element_type=F32
            ).astype(BF16)
            for chunk in range(2):
                x1_send[chunk, rows, :] = product[:, lanes(chunk, 256)]

            def block(peer_ch):
                return x1_send.at[
                    :, pl.ds(place(peer_zlo, peer_ch // 2), 16),
                    pl.ds(pl.multiple_of(peer_ch % 2 * 128, 128), 128),
                ]

            for peer_ch in others():
                send(3, 0, block(peer_ch), mine, plane(peer_zlo), peer_ch)

            @pl.when(peer_zlo == zlo)
            def _():
                keep(3, 0, block(ch), mine)

            @pl.when(peer_zlo != zlo)
            def _():
                send(3, 0, block(ch), mine, plane(peer_zlo), ch)

            return carry

        lax.fori_loop(0, 4, back, 0)

    arrive(0, 0, z_got)
    for chunk in range(2):
        for i in range(2):
            zt[chunk, :, lanes(i)] = jnp.concatenate(
                [z_got[i, lanes(part, 32), :].astype(F32) for part in range(chunk, 8, 2)],
                axis=0,
            ).T
        gate[chunk] = jax.nn.sigmoid(
            jnp.dot(wg_t[0], norm0(zt[chunk]).astype(BF16), preferred_element_type=F32)
        )

    arrive(3, 0, c1_got)

    def regroup(chunk):
        swap(c1_got.at[chunk], lambda i: c2_send.at[chunk, i])
        spread(
            4, chunk, g_peer,
            lambda peer: c2_send.at[chunk, pl.ds(peer * 2, 2)],
            c2_got.at[chunk, :, pl.ds(pl.multiple_of(g * 16, 16), 16), :],
        )

    both(regroup)

    def middle(chunk):
        arrive(4, chunk, c2_got.at[chunk])
        product = jnp.concatenate(
            [c2_got[chunk, i].astype(F32) for i in range(2)], axis=1
        )
        acc[chunk] = gate[chunk] * jnp.dot(
            wf_t[0], norm0(product).astype(BF16), preferred_element_type=F32
        )
        normed = norm0(zt[chunk] + acc[chunk]).astype(BF16)
        for side in range(2):
            value = glu(
                jnp.dot(wi_t[1, lanes(side, 256)], normed, preferred_element_type=F32)
            )
            for i in range(2):
                b1_send[chunk, side, i] = value[:, lanes(i)]
        spread(
            5, chunk, g_peer,
            lambda peer: b1_send.at[
                chunk, :, :, pl.ds(pl.multiple_of(peer * 16, 16), 16), :
            ],
            b1_got.at[chunk, :, pl.ds(g * 2, 2)],
        )

    both(middle)

    def second_to_owners(chunk):
        arrive(5, chunk, b1_got.at[chunk])
        for side in range(2):
            swap(b1_got.at[chunk, side], lambda c: b2_send.at[chunk, c, side])
        to_owners(
            6, chunk, lambda m: b2_send.at[chunk, m],
            operands.at[
                1, :, pl.ds(place(zlo, y), 16),
                pl.ds(pl.multiple_of(chunk * 256 + zhi * 128, 128), 128),
            ],
        )

    both(second_to_owners)

    for chunk in range(2):
        for i in range(2):
            total = acc[chunk, :, lanes(i)].T.astype(BF16)
            for k in range(4):
                u_send[i, lanes(2 * k + chunk, 32), :] = total[lanes(k, 32)]
    spread(
        9, 0, y_peer,
        lambda peer: u_send.at[:, pl.ds(pl.multiple_of(peer * 32, 32), 32), :],
        u_got.at[pl.ds(y * 2, 2)],
    )

    @pl.when(is_owner)
    def _():
        for chunk in range(2):
            arrive(6, chunk, operands.at[1, :, :, pl.ds(chunk * 256, 256)])
            for q in (2 * chunk, 2 * chunk + 1):
                turned[lanes(q), :] = operands[1, 1, :, lanes(q)].T
        mine = t1_got.at[ch]
        own = y % 2 * 2 + zhi

        def back(step, carry):
            part = (own + 1 + step) % 4
            rows = pl.ds(pl.multiple_of(part * 128, 128), 128)
            x2_send[rows, :] = jnp.dot(
                turned[rows, :], operands[1, 0], preferred_element_type=F32
            ).astype(BF16)

            def go(peer_zlo, k, is_self=False):
                src = x2_send.at[
                    pl.ds(pl.multiple_of(part * 128 + k * 32, 32), 32),
                    pl.ds(pl.multiple_of(peer_zlo * 128, 128), 128),
                ]
                if is_self:
                    keep(7, 0, src, mine)
                else:
                    send(7, 0, src, mine, plane(peer_zlo),
                         (2 * k + part // 2) * 2 + part % 2)

            for dk in (2, 1, 3, 0):
                for dz in (2, 1, 3, 0):
                    if dk or dz:
                        go((zlo + dz) % 4, (y // 2 + dk) % 4)

            @pl.when(part == own)
            def _():
                go(zlo, y // 2, True)

            @pl.when(part != own)
            def _():
                go(zlo, y // 2)

            return carry

        lax.fori_loop(0, 4, back, 0)

    arrive(9, 0, u_got)
    for a in range(4):
        block = z_in[lanes(a, 4)] + u_got[lanes(a, 4)].astype(F32)
        middle_t[:, lanes(a)] = block.reshape(128, 128).T
    for half in range(2):
        normed = norm0(middle_t[:, lanes(half, 256)]).astype(BF16)
        home_gate[:, lanes(half, 256)] = jax.nn.sigmoid(
            jnp.dot(wg_t[1], normed, preferred_element_type=F32)
        )

    arrive(7, 0, t1_got)
    for q in range(4):
        square[q] = t1_got[lanes(q, 4)].astype(F32).reshape(128, 128).T
    for a in range(4):
        rows = [
            jnp.concatenate(
                [square.at[q][pl.ds(4 * a + b, 8, stride=16), :] for q in range(4)], axis=0
            )
            for b in range(4)
        ]
        for t in range(4):
            mixed = jnp.concatenate([rows[b][:, lanes(t, 32)] for b in range(4)], axis=1)
            for q in range(4):
                fan[a, lanes(4 * q + t, 8)] = mixed[lanes(q, 8)]
        for peer in range(GROUP):
            t2_send[a, peer] = fan.at[a][pl.ds(peer, 16, stride=8), :].astype(BF16)
        if a % 2:
            spread(
                8, a // 2, g_peer,
                lambda peer: t2_send.at[pl.ds(a - 1, 2), peer],
                t2_got.at[pl.ds(a - 1, 2), pl.ds(pl.multiple_of(g * 16, 16), 16), :],
            )
    for half in range(2):
        arrive(8, half, t2_got.at[pl.ds(2 * half, 2)])
        product = jnp.concatenate(
            [t2_got[2 * half + n].astype(F32) for n in range(2)], axis=1
        )
        there = lanes(half, 256)
        updated = middle_t[:, there] + home_gate[:, there] * jnp.dot(
            wf_t[1], norm0(product).astype(BF16), preferred_element_type=F32
        )
        for n in range(2):
            out_ref[lanes(2 * half + n, 4)] = updated[:, lanes(n)].T.reshape(4, 32, 128)

    leave(0, z_send.at[pl.ds(0, 14)])
    leave(1, h_send.at[:, pl.ds(0, 112), :])
    leave(4, c2_send.at[:, pl.ds(0, 14)])
    leave(5, b1_send.at[:, :, :, pl.ds(0, 112), :])
    leave(8, t2_send.at[:, pl.ds(0, 7)])
    leave(9, u_send.at[:, pl.ds(0, 224), :])

    @pl.when(is_owner)
    def _():
        leave(2, k_send.at[pl.ds(0, 15)])
        leave(3, size63)
        leave(6, b2_send.at[:, pl.ds(0, 15)])
        leave(7, size63)

    @pl.when(jnp.logical_not(is_owner))
    def _():
        leave(2, k_send)
        leave(6, b2_send)


def body(pair, out_inputs, out_gate, out_final, in_inputs, in_gate, in_final):
    anywhere = pl.BlockSpec(memory_space=pl.ANY)
    return pl.pallas_call(
        kernel,
        out_shape=jax.ShapeDtypeStruct((16, 32, 128), F32),
        in_specs=[anywhere] * 7,
        out_specs=pl.BlockSpec(memory_space=pltpu.VMEM),
        scratch_shapes=[
            pltpu.VMEM((16, 32, 128), F32),
            pltpu.VMEM((2, 128, 512), BF16),
            pltpu.VMEM((2, 128, 128), BF16),
            pltpu.VMEM((2, 128, 128), BF16),
            pltpu.VMEM((16, 32, 128), BF16),
            pltpu.VMEM((2, 256, 128), BF16),
            pltpu.VMEM((2, 512, 128), BF16),
            pltpu.VMEM((2, 128, 128), BF16),
            pltpu.VMEM((2, 128, 128), BF16),
            pltpu.VMEM((2, 128, 256), F32),
            pltpu.VMEM((2, 128, 256), F32),
            pltpu.VMEM((2, 128, 256), F32),
            pltpu.VMEM((2, 128, 512), BF16),
            pltpu.VMEM((2, 8, 16, 512), BF16),
            pltpu.VMEM((4, 128, 128), F32),
            pltpu.VMEM((4, 128, 128), F32),
            pltpu.VMEM((16, 2, 32, 128), BF16),
            pltpu.VMEM((2, 2, 2, 128, 128), BF16),
            pltpu.VMEM((2, 2, 16, 16, 128), BF16),
            pltpu.VMEM((256, 128), F32),
            pltpu.VMEM((2, 16, 2, 16, 128), BF16),
            pltpu.VMEM((2, 2, 512, 512), BF16),
            pltpu.VMEM((2, 512, 256), BF16),
            pltpu.VMEM((2, 16, 16, 128), BF16),
            pltpu.VMEM((2, 16, 16, 128), BF16),
            pltpu.VMEM((2, 2, 128, 128), BF16),
            pltpu.VMEM((512, 512), BF16),
            pltpu.VMEM((16, 32, 128), BF16),
            pltpu.VMEM((4, 8, 16, 128), BF16),
            pltpu.VMEM((4, 128, 128), BF16),
            pltpu.VMEM((2, 256, 128), BF16),
            pltpu.VMEM((16, 32, 128), BF16),
            pltpu.VMEM((128, 512), F32),
            pltpu.VMEM((128, 512), F32),
            pltpu.VMEM((512, 512), BF16),
            pltpu.VMEM((1008, 256), BF16),
            pltpu.SemaphoreType.DMA((PHASES,)),
            pltpu.SemaphoreType.DMA((PHASES, 2)),
            pltpu.SemaphoreType.DMA((7,)),
            pltpu.SemaphoreType.REGULAR,
        ],
        compiler_params=pltpu.CompilerParams(
            collective_id=0, has_side_effects=True, vmem_limit_bytes=60 * 1024 * 1024
        ),
        name="triangles",
    )(pair, out_inputs, out_gate, out_final, in_inputs, in_gate, in_final)


def solution(mesh):
    placed = (P("row", "ch", None), P(), P(), P(), P(), P(), P())
    return jax.shard_map(
        body, mesh=mesh, in_specs=placed, out_specs=P("row", "ch", None), check_vma=False
    )
```

```python
import jax
import jax.numpy as jnp
from jax import lax
from jax.experimental import pallas as pl
from jax.experimental.pallas import tpu as pltpu
from jax.sharding import PartitionSpec as P

MESH = pl.DeviceIdType.MESH
BF16 = jnp.bfloat16
F32 = jnp.float32
GROUP = 8
OWNERS = 16
FAR_FIRST = (4, 3, 5, 2, 6, 1, 7)
PHASES = 10


def norm0(values):
    mean = jnp.mean(values, axis=0, keepdims=True)
    centered = values - mean
    variance = jnp.mean(centered * centered, axis=0, keepdims=True)
    return centered * lax.rsqrt(variance + 1e-05)


def flip(w):
    return w.astype(F32).T.astype(BF16)


def place(zlo, y):
    return pl.multiple_of(zlo * 128 + y * 16, 16)


def kernel(
    z_hbm, wi0, wg0, wf0, wi1, wg1, wf1, out_ref,
    z_in, wi_in, wg_in, wf_in, z_send, z_got, wi_t, wg_t, wf_t, zt, acc, gate,
    h_send, h_got, fan, square, k_send, b1_send, b1_got, turn, b2_send, operands,
    x1_send, c1_got, c2_send, c2_got, x2_send, t1_got, t2_send, t2_got,
    u_send, u_got, middle_t, home_gate, turned, size63, send_sem, recv_sem, in_sem, ready,
):
    row = lax.axis_index("row")
    ch = lax.axis_index("ch")
    y, zhi = ch // 2, ch % 2
    x, zlo, core = row // 8, row % 8 // 2, row % 2
    g = x * 2 + core

    def owner_zlo(m):
        return m // 2 % 2 + 2 * ((m // 4 + core) % 2)

    def plane(peer_zlo):
        return x * 8 + peer_zlo * 2 + core

    is_owner = zlo == owner_zlo(ch)

    def send(phase, chunk, src, dst, to_row, to_ch):
        pltpu.make_async_remote_copy(
            src_ref=src, dst_ref=dst,
            send_sem=send_sem.at[phase], recv_sem=recv_sem.at[phase, chunk],
            device_id=(to_row, to_ch), device_id_type=MESH,
        ).start()

    def keep(phase, chunk, src, dst):
        pltpu.make_async_copy(src, dst, recv_sem.at[phase, chunk]).start()

    def arrive(phase, chunk, ref):
        pltpu.make_async_copy(ref, ref, recv_sem.at[phase, chunk]).wait()

    def leave(phase, ref):
        pltpu.make_async_copy(ref, ref, send_sem.at[phase]).wait()

    def y_peer(step):
        peer = (y + step) % GROUP
        return peer, row, peer * 2 + zhi

    def g_peer(step):
        peer = (g + step) % GROUP
        return peer, peer // 2 * 8 + zlo * 2 + peer % 2, ch

    def z_peer(step):
        peer = (zhi * 4 + zlo + step) % GROUP
        return peer, plane(peer % 4), y * 2 + peer // 4

    def spread(phase, chunk, peer_of, src_of, dst):
        for step in FAR_FIRST:
            peer, to_row, to_ch = peer_of(step)
            send(phase, chunk, src_of(peer), dst, to_row, to_ch)
        keep(phase, chunk, src_of(peer_of(0)[0]), dst)

    def others():
        for dy in (*FAR_FIRST, 0):
            for dz in (1, 0):
                if dy or dz:
                    yield (y + dy) % 8 * 2 + (zhi + dz) % 2

    def to_owners(phase, chunk, src_of, here):
        for m in others():
            send(phase, chunk, src_of(m), here, plane(owner_zlo(m)), m)

        @pl.when(is_owner)
        def _():
            keep(phase, chunk, src_of(ch), here)

        @pl.when(jnp.logical_not(is_owner))
        def _():
            send(phase, chunk, src_of(ch), here, plane(owner_zlo(ch)), ch)

    def both(stage):
        def one(chunk, carry):
            stage(chunk)
            return carry

        lax.fori_loop(0, 2, one, 0)

    def swap(src, dst_of):
        turn[...] = src[...].astype(F32).reshape(256, 128)
        for b in range(16):
            dst_of(b)[...] = turn[pl.ds(b, 16, stride=16), :].astype(BF16)

    def lanes(n, width=128):
        return slice(n * width, (n + 1) * width)

    def glu(proj):
        return (jax.nn.sigmoid(proj[128:]) * proj[:128]).astype(BF16)

    weights = ((wi0, wi_in.at[0]), (wg0, wg_in.at[0]), (wf0, wf_in.at[0]),
               (wi1, wi_in.at[1]), (wg1, wg_in.at[1]), (wf1, wf_in.at[1]))
    loads = [
        pltpu.make_async_copy(src, dst, in_sem.at[n])
        for n, (src, dst) in enumerate(((z_hbm, z_in), *weights))
    ]
    for load in loads:
        load.start()

    barrier = pltpu.get_barrier_semaphore()
    for line in (y_peer, g_peer, z_peer):
        for step in range(1, GROUP):
            _, to_row, to_ch = line(step)
            pl.semaphore_signal(
                barrier, inc=1, device_id=(to_row, to_ch), device_id_type=MESH
            )
    loads[1].wait()
    wi_t[0] = flip(wi_in[0])
    loads[0].wait()
    zn = jnp.concatenate(
        [norm0(z_in[4 * a:4 * a + 4].reshape(128, 128).T).astype(BF16) for a in range(4)],
        axis=1,
    )
    for side in range(2):
        h_send[side] = glu(
            jnp.dot(wi_t[0, lanes(side, 256)], zn, preferred_element_type=F32)
        )
        if side == 0:
            pl.semaphore_wait(barrier, 3 * (GROUP - 1))
            for step in FAR_FIRST:
                _, to_row, to_ch = y_peer(step)
                pl.semaphore_signal(
                    ready, inc=1, device_id=(to_row, to_ch), device_id_type=MESH
                )
        spread(
            1, side, g_peer,
            lambda peer: h_send.at[side, pl.ds(pl.multiple_of(peer * 16, 16), 16), :],
            h_got.at[side, g],
        )
    z_send[...] = z_in[...].astype(BF16)
    spread(
        0, 0, y_peer,
        lambda peer: z_send.at[pl.ds(peer * 2, 2)],
        z_got.at[:, pl.ds(pl.multiple_of(y * 32, 32), 32), :],
    )
    pl.semaphore_wait(ready, GROUP - 1)

    for side in range(2):
        arrive(1, side, h_got.at[side])
        for a in range(4):
            for peer in range(GROUP):
                fan.at[a][pl.ds(peer, 16, stride=8), :] = h_got[
                    side, peer, :, lanes(a)
                ].astype(F32)
            rows = fan[a].reshape(4, 4, 8, 128)
            for b in range(4):
                i = 4 * a + b
                start, stride = (i // 2 * 16 + i % 2, 2) if side == 0 else (i, 16)
                mixed = jnp.concatenate(
                    [rows[:, t].reshape(32, 128)[:, lanes(b, 32)] for t in range(4)], axis=1
                )
                for q in range(4):
                    square.at[q][pl.ds(start, 8, stride=stride), :] = mixed[lanes(q, 8)]
        for q in range(4):
            k_send[4 * q:4 * q + 4, side] = square[q].T.reshape(4, 32, 128).astype(BF16)
        to_owners(
            2, side, lambda m: k_send.at[m, side],
            operands.at[
                0, side, pl.ds(pl.multiple_of(ch * 32, 32), 32),
                pl.ds(pl.multiple_of(zlo * 128, 128), 128),
            ],
        )

    for load in loads[2:]:
        load.wait()
    wi_t[1] = flip(wi_in[1])
    for u in range(2):
        wg_t[u] = flip(wg_in[u])
        wf_t[u] = flip(wf_in[u])

    arrive(0, 0, z_got)
    for chunk in range(2):
        for i in range(2):
            zt[chunk, :, lanes(i)] = jnp.concatenate(
                [z_got[i, lanes(part, 32), :].astype(F32) for part in range(chunk, 8, 2)],
                axis=0,
            ).T
        gate[chunk] = jax.nn.sigmoid(
            jnp.dot(wg_t[0], norm0(zt[chunk]).astype(BF16), preferred_element_type=F32)
        )

    @pl.when(is_owner)
    def _():
        arrive(2, 0, operands.at[0, 0])
        for q in range(4):
            turned[lanes(q), :] = operands[0, 0, :, lanes(q)].T
        arrive(2, 1, operands.at[0, 1])

        def back(step, carry):
            chunk = step // 4
            peer_zlo = (zlo + 1 + step) % 4
            rows = pl.ds(pl.multiple_of(peer_zlo * 128, 128), 128)
            columns = pl.ds(pl.multiple_of(chunk * 256, 256), 256)
            x1_send[chunk, rows, :] = jnp.dot(
                turned[rows, :], operands[0, 1, :, columns], preferred_element_type=F32
            ).astype(BF16)
            mine = c1_got.at[chunk, ch]

            def block(peer_ch):
                return x1_send.at[
                    chunk, pl.ds(place(peer_zlo, peer_ch // 2), 16),
                    pl.ds(pl.multiple_of(peer_ch % 2 * 128, 128), 128),
                ]

            for peer_ch in others():
                send(3, chunk, block(peer_ch), mine, plane(peer_zlo), peer_ch)

            @pl.when(peer_zlo == zlo)
            def _():
                keep(3, chunk, block(ch), mine)

            @pl.when(peer_zlo != zlo)
            def _():
                send(3, chunk, block(ch), mine, plane(peer_zlo), ch)

            return carry

        lax.fori_loop(0, 8, back, 0)

    def regroup(chunk):
        arrive(3, chunk, c1_got.at[chunk])
        swap(c1_got.at[chunk], lambda i: c2_send.at[chunk, i])
        spread(
            4, chunk, g_peer,
            lambda peer: c2_send.at[chunk, pl.ds(peer * 2, 2)],
            c2_got.at[chunk, :, pl.ds(pl.multiple_of(g * 16, 16), 16), :],
        )

    both(regroup)

    def middle(chunk):
        arrive(4, chunk, c2_got.at[chunk])
        product = jnp.concatenate(
            [c2_got[chunk, i].astype(F32) for i in range(2)], axis=1
        )
        acc[chunk] = gate[chunk] * jnp.dot(
            wf_t[0], norm0(product).astype(BF16), preferred_element_type=F32
        )
        normed = norm0(zt[chunk] + acc[chunk]).astype(BF16)
        for side in range(2):
            value = glu(
                jnp.dot(wi_t[1, lanes(side, 256)], normed, preferred_element_type=F32)
            )
            for i in range(2):
                b1_send[chunk, side, i] = value[:, lanes(i)]
        spread(
            5, chunk, g_peer,
            lambda peer: b1_send.at[
                chunk, :, :, pl.ds(pl.multiple_of(peer * 16, 16), 16), :
            ],
            b1_got.at[chunk, :, pl.ds(g * 2, 2)],
        )

    both(middle)

    def second_to_owners(chunk):
        arrive(5, chunk, b1_got.at[chunk])
        for side in range(2):
            swap(b1_got.at[chunk, side], lambda c: b2_send.at[chunk, c, side])
        to_owners(
            6, chunk, lambda m: b2_send.at[chunk, m],
            operands.at[
                1, :, pl.ds(place(zlo, y), 16),
                pl.ds(pl.multiple_of(chunk * 256 + zhi * 128, 128), 128),
            ],
        )

    both(second_to_owners)

    for chunk in range(2):
        for i in range(2):
            total = acc[chunk, :, lanes(i)].T.astype(BF16)
            for k in range(4):
                u_send[i, lanes(2 * k + chunk, 32), :] = total[lanes(k, 32)]
    spread(
        9, 0, y_peer,
        lambda peer: u_send.at[:, pl.ds(pl.multiple_of(peer * 32, 32), 32), :],
        u_got.at[pl.ds(y * 2, 2)],
    )

    @pl.when(is_owner)
    def _():
        for chunk in range(2):
            arrive(6, chunk, operands.at[1, :, :, pl.ds(chunk * 256, 256)])
            for q in (2 * chunk, 2 * chunk + 1):
                turned[lanes(q), :] = operands[1, 1, :, lanes(q)].T
        mine = t1_got.at[ch]
        own = (y % 2 * 2 + zhi) * 2 + zlo // 2

        def back(step, carry):
            place_of = (own + 1 + step) % 8
            part, side = place_of // 2, place_of % 2
            rows = pl.ds(pl.multiple_of(part * 128, 128), 128)
            columns = pl.ds(pl.multiple_of(side * 256, 256), 256)
            x2_send[rows, columns] = jnp.dot(
                turned[rows, :], operands[1, 0, :, columns], preferred_element_type=F32
            ).astype(BF16)

            def go(peer_zlo, k, is_self=False):
                src = x2_send.at[
                    pl.ds(pl.multiple_of(part * 128 + k * 32, 32), 32),
                    pl.ds(pl.multiple_of(peer_zlo * 128, 128), 128),
                ]
                if is_self:
                    keep(7, 0, src, mine)
                else:
                    send(7, 0, src, mine, plane(peer_zlo),
                         (2 * k + part // 2) * 2 + part % 2)

            for dk in (2, 1, 3, 0):
                for dz in (1, 0):
                    if dk or dz:
                        go(side * 2 + (zlo + dz) % 2, (y // 2 + dk) % 4)

            @pl.when(place_of == own)
            def _():
                go(zlo, y // 2, True)

            @pl.when(place_of != own)
            def _():
                go(side * 2 + zlo % 2, y // 2)

            return carry

        lax.fori_loop(0, 8, back, 0)

    arrive(7, 0, t1_got)
    for q in range(4):
        square[q] = t1_got[lanes(q, 4)].astype(F32).reshape(128, 128).T
    for a in range(4):
        rows = [
            jnp.concatenate(
                [square.at[q][pl.ds(4 * a + b, 8, stride=16), :] for q in range(4)], axis=0
            )
            for b in range(4)
        ]
        for t in range(4):
            mixed = jnp.concatenate([rows[b][:, lanes(t, 32)] for b in range(4)], axis=1)
            for q in range(4):
                fan[a, lanes(4 * q + t, 8)] = mixed[lanes(q, 8)]
        for peer in range(GROUP):
            t2_send[a, peer] = fan.at[a][pl.ds(peer, 16, stride=8), :].astype(BF16)
        if a % 2:
            spread(
                8, a // 2, g_peer,
                lambda peer: t2_send.at[pl.ds(a - 1, 2), peer],
                t2_got.at[pl.ds(a - 1, 2), pl.ds(pl.multiple_of(g * 16, 16), 16), :],
            )
    arrive(9, 0, u_got)
    for a in range(4):
        block = z_in[lanes(a, 4)] + u_got[lanes(a, 4)].astype(F32)
        middle_t[:, lanes(a)] = block.reshape(128, 128).T
    for half in range(2):
        normed = norm0(middle_t[:, lanes(half, 256)]).astype(BF16)
        home_gate[:, lanes(half, 256)] = jax.nn.sigmoid(
            jnp.dot(wg_t[1], normed, preferred_element_type=F32)
        )

    for half in range(2):
        arrive(8, half, t2_got.at[pl.ds(2 * half, 2)])
        product = jnp.concatenate(
            [t2_got[2 * half + n].astype(F32) for n in range(2)], axis=1
        )
        there = lanes(half, 256)
        updated = middle_t[:, there] + home_gate[:, there] * jnp.dot(
            wf_t[1], norm0(product).astype(BF16), preferred_element_type=F32
        )
        for n in range(2):
            out_ref[lanes(2 * half + n, 4)] = updated[:, lanes(n)].T.reshape(4, 32, 128)

    leave(0, z_send.at[pl.ds(0, 14)])
    leave(1, h_send.at[:, pl.ds(0, 112), :])
    leave(4, c2_send.at[:, pl.ds(0, 14)])
    leave(5, b1_send.at[:, :, :, pl.ds(0, 112), :])
    leave(8, t2_send.at[:, pl.ds(0, 7)])
    leave(9, u_send.at[:, pl.ds(0, 224), :])

    @pl.when(is_owner)
    def _():
        leave(2, k_send.at[pl.ds(0, 15)])
        leave(3, size63)
        leave(6, b2_send.at[:, pl.ds(0, 15)])
        leave(7, size63)

    @pl.when(jnp.logical_not(is_owner))
    def _():
        leave(2, k_send)
        leave(6, b2_send)


def body(pair, out_inputs, out_gate, out_final, in_inputs, in_gate, in_final):
    anywhere = pl.BlockSpec(memory_space=pl.ANY)
    return pl.pallas_call(
        kernel,
        out_shape=jax.ShapeDtypeStruct((16, 32, 128), F32),
        in_specs=[anywhere] * 7,
        out_specs=pl.BlockSpec(memory_space=pltpu.VMEM),
        scratch_shapes=[
            pltpu.VMEM((16, 32, 128), F32),
            pltpu.VMEM((2, 128, 512), BF16),
            pltpu.VMEM((2, 128, 128), BF16),
            pltpu.VMEM((2, 128, 128), BF16),
            pltpu.VMEM((16, 32, 128), BF16),
            pltpu.VMEM((2, 256, 128), BF16),
            pltpu.VMEM((2, 512, 128), BF16),
            pltpu.VMEM((2, 128, 128), BF16),
            pltpu.VMEM((2, 128, 128), BF16),
            pltpu.VMEM((2, 128, 256), F32),
            pltpu.VMEM((2, 128, 256), F32),
            pltpu.VMEM((2, 128, 256), F32),
            pltpu.VMEM((2, 128, 512), BF16),
            pltpu.VMEM((2, 8, 16, 512), BF16),
            pltpu.VMEM((4, 128, 128), F32),
            pltpu.VMEM((4, 128, 128), F32),
            pltpu.VMEM((16, 2, 32, 128), BF16),
            pltpu.VMEM((2, 2, 2, 128, 128), BF16),
            pltpu.VMEM((2, 2, 16, 16, 128), BF16),
            pltpu.VMEM((256, 128), F32),
            pltpu.VMEM((2, 16, 2, 16, 128), BF16),
            pltpu.VMEM((2, 2, 512, 512), BF16),
            pltpu.VMEM((2, 512, 256), BF16),
            pltpu.VMEM((2, 16, 16, 128), BF16),
            pltpu.VMEM((2, 16, 16, 128), BF16),
            pltpu.VMEM((2, 2, 128, 128), BF16),
            pltpu.VMEM((512, 512), BF16),
            pltpu.VMEM((16, 32, 128), BF16),
            pltpu.VMEM((4, 8, 16, 128), BF16),
            pltpu.VMEM((4, 128, 128), BF16),
            pltpu.VMEM((2, 256, 128), BF16),
            pltpu.VMEM((16, 32, 128), BF16),
            pltpu.VMEM((128, 512), F32),
            pltpu.VMEM((128, 512), F32),
            pltpu.VMEM((512, 512), BF16),
            pltpu.VMEM((1008, 256), BF16),
            pltpu.SemaphoreType.DMA((PHASES,)),
            pltpu.SemaphoreType.DMA((PHASES, 2)),
            pltpu.SemaphoreType.DMA((7,)),
            pltpu.SemaphoreType.REGULAR,
        ],
        compiler_params=pltpu.CompilerParams(
            collective_id=0, has_side_effects=True, vmem_limit_bytes=60 * 1024 * 1024
        ),
        name="triangles",
    )(pair, out_inputs, out_gate, out_final, in_inputs, in_gate, in_final)


def solution(mesh):
    placed = (P("row", "ch", None), P(), P(), P(), P(), P(), P())
    return jax.shard_map(
        body, mesh=mesh, in_specs=placed, out_specs=P("row", "ch", None), check_vma=False
    )
```

```python
import jax
import jax.numpy as jnp
from jax import lax
from jax.experimental import pallas as pl
from jax.experimental.pallas import tpu as pltpu
from jax.sharding import PartitionSpec as P

MESH = pl.DeviceIdType.MESH
BF16 = jnp.bfloat16
F32 = jnp.float32
GROUP = 8
OWNERS = 16
FAR_FIRST = (4, 3, 5, 2, 6, 1, 7)
PHASES = 10


def norm0(values):
    mean = jnp.mean(values, axis=0, keepdims=True)
    centered = values - mean
    variance = jnp.mean(centered * centered, axis=0, keepdims=True)
    return centered * lax.rsqrt(variance + 1e-05)


def flip(w):
    return w.astype(F32).T.astype(BF16)


def place(zlo, y):
    return pl.multiple_of(zlo * 128 + y * 16, 16)


def kernel(
    z_hbm, wi0, wg0, wf0, wi1, wg1, wf1, out_ref,
    z_in, wi_in, wg_in, wf_in, z_send, z_got, wi_t, wg_t, wf_t, zt, acc, gate,
    h_send, h_got, fan, square, k_send, b1_send, b1_got, turn, b2_send, operands,
    x1_send, c1_got, c2_send, c2_got, x2_send, t1_got, t2_send, t2_got,
    u_send, u_got, middle_t, home_gate, turned, size63, send_sem, recv_sem, in_sem, ready,
):
    row = lax.axis_index("row")
    ch = lax.axis_index("ch")
    y, zhi = ch // 2, ch % 2
    x, zlo, core = row // 8, row % 8 // 2, row % 2
    g = x * 2 + core

    def owner_zlo(m):
        return m // 2 % 2 + 2 * ((m // 4 + core) % 2)

    def plane(peer_zlo):
        return x * 8 + peer_zlo * 2 + core

    is_owner = zlo == owner_zlo(ch)

    def send(phase, chunk, src, dst, to_row, to_ch):
        pltpu.make_async_remote_copy(
            src_ref=src, dst_ref=dst,
            send_sem=send_sem.at[phase], recv_sem=recv_sem.at[phase, chunk],
            device_id=(to_row, to_ch), device_id_type=MESH,
        ).start()

    def keep(phase, chunk, src, dst):
        pltpu.make_async_copy(src, dst, recv_sem.at[phase, chunk]).start()

    def arrive(phase, chunk, ref):
        pltpu.make_async_copy(ref, ref, recv_sem.at[phase, chunk]).wait()

    def leave(phase, ref):
        pltpu.make_async_copy(ref, ref, send_sem.at[phase]).wait()

    def y_peer(step):
        peer = (y + step) % GROUP
        return peer, row, peer * 2 + zhi

    def g_peer(step):
        peer = (g + step) % GROUP
        return peer, peer // 2 * 8 + zlo * 2 + peer % 2, ch

    def z_peer(step):
        peer = (zhi * 4 + zlo + step) % GROUP
        return peer, plane(peer % 4), y * 2 + peer // 4

    def spread(phase, chunk, peer_of, src_of, dst):
        for step in FAR_FIRST:
            peer, to_row, to_ch = peer_of(step)
            send(phase, chunk, src_of(peer), dst, to_row, to_ch)
        keep(phase, chunk, src_of(peer_of(0)[0]), dst)

    def others():
        for dy in (*FAR_FIRST, 0):
            for dz in (1, 0):
                if dy or dz:
                    yield (y + dy) % 8 * 2 + (zhi + dz) % 2

    def to_owners(phase, chunk, src_of, here, turn_of):
        for dy in (*FAR_FIRST, 0):
            peer_y = (y + dy) % 8
            m = peer_y * 2 + (peer_y // 2 + turn_of) % 2
            if dy:
                send(phase, chunk, src_of(m), here, plane(owner_zlo(m)), m)
        own = jnp.logical_and(is_owner, m == ch)

        @pl.when(own)
        def _():
            keep(phase, chunk, src_of(ch), here)

        @pl.when(jnp.logical_not(own))
        def _():
            send(phase, chunk, src_of(m), here, plane(owner_zlo(m)), m)

    def both(stage):
        def one(chunk, carry):
            stage(chunk)
            return carry

        lax.fori_loop(0, 2, one, 0)

    def swap(src, dst_of):
        turn[...] = src[...].astype(F32).reshape(256, 128)
        for b in range(16):
            dst_of(b)[...] = turn[pl.ds(b, 16, stride=16), :].astype(BF16)

    def lanes(n, width=128):
        return slice(n * width, (n + 1) * width)

    def glu(proj):
        return (jax.nn.sigmoid(proj[128:]) * proj[:128]).astype(BF16)

    weights = ((wi0, wi_in.at[0]), (wg0, wg_in.at[0]), (wf0, wf_in.at[0]),
               (wi1, wi_in.at[1]), (wg1, wg_in.at[1]), (wf1, wf_in.at[1]))
    loads = [
        pltpu.make_async_copy(src, dst, in_sem.at[n])
        for n, (src, dst) in enumerate(((z_hbm, z_in), *weights))
    ]
    for load in loads:
        load.start()

    barrier = pltpu.get_barrier_semaphore()
    for line in (y_peer, g_peer, z_peer):
        for step in range(1, GROUP):
            _, to_row, to_ch = line(step)
            pl.semaphore_signal(
                barrier, inc=1, device_id=(to_row, to_ch), device_id_type=MESH
            )
    loads[1].wait()
    wi_t[0] = flip(wi_in[0])
    loads[0].wait()
    zn = jnp.concatenate(
        [norm0(z_in[4 * a:4 * a + 4].reshape(128, 128).T).astype(BF16) for a in range(4)],
        axis=1,
    )
    for side in range(2):
        h_send[side] = glu(
            jnp.dot(wi_t[0, lanes(side, 256)], zn, preferred_element_type=F32)
        )
        if side == 0:
            pl.semaphore_wait(barrier, 3 * (GROUP - 1))
            for step in FAR_FIRST:
                _, to_row, to_ch = y_peer(step)
                pl.semaphore_signal(
                    ready, inc=1, device_id=(to_row, to_ch), device_id_type=MESH
                )
        spread(
            1, side, g_peer,
            lambda peer: h_send.at[side, pl.ds(pl.multiple_of(peer * 16, 16), 16), :],
            h_got.at[side, g],
        )
    pl.semaphore_wait(ready, GROUP - 1)

    def first_to_owners(side, turn_of):
        to_owners(
            2, side, lambda m: k_send.at[m, side],
            operands.at[
                0, side, pl.ds(pl.multiple_of(ch * 32, 32), 32),
                pl.ds(pl.multiple_of(zlo * 128, 128), 128),
            ],
            turn_of,
        )

    for side in range(2):
        arrive(1, side, h_got.at[side])
        for a in range(4):
            for peer in range(GROUP):
                fan.at[a][pl.ds(peer, 16, stride=8), :] = h_got[
                    side, peer, :, lanes(a)
                ].astype(F32)
            rows = fan[a].reshape(4, 4, 8, 128)
            for b in range(4):
                i = 4 * a + b
                start, stride = (i // 2 * 16 + i % 2, 2) if side == 0 else (i, 16)
                mixed = jnp.concatenate(
                    [rows[:, t].reshape(32, 128)[:, lanes(b, 32)] for t in range(4)], axis=1
                )
                for q in range(4):
                    square.at[q][pl.ds(start, 8, stride=stride), :] = mixed[lanes(q, 8)]
        for q in range(4):
            k_send[4 * q:4 * q + 4, side] = square[q].T.reshape(4, 32, 128).astype(BF16)
        first_to_owners(side, 0)
    for side in range(2):
        first_to_owners(side, 1)

    z_send[...] = z_in[...].astype(BF16)
    spread(
        0, 0, y_peer,
        lambda peer: z_send.at[pl.ds(peer * 2, 2)],
        z_got.at[:, pl.ds(pl.multiple_of(y * 32, 32), 32), :],
    )
    for load in loads[2:]:
        load.wait()
    wi_t[1] = flip(wi_in[1])
    for u in range(2):
        wg_t[u] = flip(wg_in[u])
        wf_t[u] = flip(wf_in[u])

    @pl.when(is_owner)
    def _():
        arrive(2, 0, operands.at[0, 0])
        for q in range(4):
            turned[lanes(q), :] = operands[0, 0, :, lanes(q)].T
        arrive(2, 1, operands.at[0, 1])

        def back(step, carry):
            chunk = step // 4
            peer_zlo = (zlo + 1 + step) % 4
            rows = pl.ds(pl.multiple_of(peer_zlo * 128, 128), 128)
            columns = pl.ds(pl.multiple_of(chunk * 256, 256), 256)
            x1_send[chunk, rows, :] = jnp.dot(
                turned[rows, :], operands[0, 1, :, columns], preferred_element_type=F32
            ).astype(BF16)
            mine = c1_got.at[chunk, ch]

            def block(peer_ch):
                return x1_send.at[
                    chunk, pl.ds(place(peer_zlo, peer_ch // 2), 16),
                    pl.ds(pl.multiple_of(peer_ch % 2 * 128, 128), 128),
                ]

            for peer_ch in others():
                send(3, chunk, block(peer_ch), mine, plane(peer_zlo), peer_ch)

            @pl.when(peer_zlo == zlo)
            def _():
                keep(3, chunk, block(ch), mine)

            @pl.when(peer_zlo != zlo)
            def _():
                send(3, chunk, block(ch), mine, plane(peer_zlo), ch)

            return carry

        lax.fori_loop(0, 8, back, 0)

    arrive(0, 0, z_got)
    for chunk in range(2):
        for i in range(2):
            zt[chunk, :, lanes(i)] = jnp.concatenate(
                [z_got[i, lanes(part, 32), :].astype(F32) for part in range(chunk, 8, 2)],
                axis=0,
            ).T
        gate[chunk] = jax.nn.sigmoid(
            jnp.dot(wg_t[0], norm0(zt[chunk]).astype(BF16), preferred_element_type=F32)
        )

    def regroup(chunk):
        arrive(3, chunk, c1_got.at[chunk])
        swap(c1_got.at[chunk], lambda i: c2_send.at[chunk, i])
        spread(
            4, chunk, g_peer,
            lambda peer: c2_send.at[chunk, pl.ds(peer * 2, 2)],
            c2_got.at[chunk, :, pl.ds(pl.multiple_of(g * 16, 16), 16), :],
        )

    both(regroup)

    def middle(chunk):
        arrive(4, chunk, c2_got.at[chunk])
        product = jnp.concatenate(
            [c2_got[chunk, i].astype(F32) for i in range(2)], axis=1
        )
        acc[chunk] = gate[chunk] * jnp.dot(
            wf_t[0], norm0(product).astype(BF16), preferred_element_type=F32
        )
        normed = norm0(zt[chunk] + acc[chunk]).astype(BF16)
        for side in range(2):
            value = glu(
                jnp.dot(wi_t[1, lanes(side, 256)], normed, preferred_element_type=F32)
            )
            for i in range(2):
                b1_send[chunk, side, i] = value[:, lanes(i)]
        spread(
            5, chunk, g_peer,
            lambda peer: b1_send.at[
                chunk, :, :, pl.ds(pl.multiple_of(peer * 16, 16), 16), :
            ],
            b1_got.at[chunk, :, pl.ds(g * 2, 2)],
        )

    both(middle)

    def second_to_owners(chunk):
        arrive(5, chunk, b1_got.at[chunk])
        for side in range(2):
            swap(b1_got.at[chunk, side], lambda c: b2_send.at[chunk, c, side])
        for turn_of in range(2):
            to_owners(
                6, chunk, lambda m: b2_send.at[chunk, m],
                operands.at[
                    1, :, pl.ds(place(zlo, y), 16),
                    pl.ds(pl.multiple_of(chunk * 256 + zhi * 128, 128), 128),
                ],
                turn_of,
            )

    both(second_to_owners)

    for chunk in range(2):
        for i in range(2):
            total = acc[chunk, :, lanes(i)].T.astype(BF16)
            for k in range(4):
                u_send[i, lanes(2 * k + chunk, 32), :] = total[lanes(k, 32)]
    spread(
        9, 0, y_peer,
        lambda peer: u_send.at[:, pl.ds(pl.multiple_of(peer * 32, 32), 32), :],
        u_got.at[pl.ds(y * 2, 2)],
    )

    @pl.when(is_owner)
    def _():
        for chunk in range(2):
            arrive(6, chunk, operands.at[1, :, :, pl.ds(chunk * 256, 256)])
            for q in (2 * chunk, 2 * chunk + 1):
                turned[lanes(q), :] = operands[1, 1, :, lanes(q)].T
        mine = t1_got.at[ch]
        own = y % 2 * 2 + zhi

        def back(step, carry):
            part = (own + 1 + step) % 4
            rows = pl.ds(pl.multiple_of(part * 128, 128), 128)
            x2_send[rows, :] = jnp.dot(
                turned[rows, :], operands[1, 0], preferred_element_type=F32
            ).astype(BF16)

            def go(peer_zlo, k, is_self=False):
                src = x2_send.at[
                    pl.ds(pl.multiple_of(part * 128 + k * 32, 32), 32),
                    pl.ds(pl.multiple_of(peer_zlo * 128, 128), 128),
                ]
                if is_self:
                    keep(7, 0, src, mine)
                else:
                    send(7, 0, src, mine, plane(peer_zlo),
                         (2 * k + part // 2) * 2 + part % 2)

            for dk in (2, 1, 3, 0):
                for dz in (2, 1, 3, 0):
                    if dk or dz:
                        go((zlo + dz) % 4, (y // 2 + dk) % 4)

            @pl.when(part == own)
            def _():
                go(zlo, y // 2, True)

            @pl.when(part != own)
            def _():
                go(zlo, y // 2)

            return carry

        lax.fori_loop(0, 4, back, 0)

    arrive(9, 0, u_got)
    for a in range(4):
        block = z_in[lanes(a, 4)] + u_got[lanes(a, 4)].astype(F32)
        middle_t[:, lanes(a)] = block.reshape(128, 128).T
    for half in range(2):
        normed = norm0(middle_t[:, lanes(half, 256)]).astype(BF16)
        home_gate[:, lanes(half, 256)] = jax.nn.sigmoid(
            jnp.dot(wg_t[1], normed, preferred_element_type=F32)
        )

    arrive(7, 0, t1_got)
    for q in range(4):
        square[q] = t1_got[lanes(q, 4)].astype(F32).reshape(128, 128).T
    for a in range(4):
        rows = [
            jnp.concatenate(
                [square.at[q][pl.ds(4 * a + b, 8, stride=16), :] for q in range(4)], axis=0
            )
            for b in range(4)
        ]
        for t in range(4):
            mixed = jnp.concatenate([rows[b][:, lanes(t, 32)] for b in range(4)], axis=1)
            for q in range(4):
                fan[a, lanes(4 * q + t, 8)] = mixed[lanes(q, 8)]
        for peer in range(GROUP):
            t2_send[a, peer] = fan.at[a][pl.ds(peer, 16, stride=8), :].astype(BF16)
        if a % 2:
            spread(
                8, a // 2, g_peer,
                lambda peer: t2_send.at[pl.ds(a - 1, 2), peer],
                t2_got.at[pl.ds(a - 1, 2), pl.ds(pl.multiple_of(g * 16, 16), 16), :],
            )
    for half in range(2):
        arrive(8, half, t2_got.at[pl.ds(2 * half, 2)])
        product = jnp.concatenate(
            [t2_got[2 * half + n].astype(F32) for n in range(2)], axis=1
        )
        there = lanes(half, 256)
        updated = middle_t[:, there] + home_gate[:, there] * jnp.dot(
            wf_t[1], norm0(product).astype(BF16), preferred_element_type=F32
        )
        for n in range(2):
            out_ref[lanes(2 * half + n, 4)] = updated[:, lanes(n)].T.reshape(4, 32, 128)

    leave(0, z_send.at[pl.ds(0, 14)])
    leave(1, h_send.at[:, pl.ds(0, 112), :])
    leave(4, c2_send.at[:, pl.ds(0, 14)])
    leave(5, b1_send.at[:, :, :, pl.ds(0, 112), :])
    leave(8, t2_send.at[:, pl.ds(0, 7)])
    leave(9, u_send.at[:, pl.ds(0, 224), :])

    @pl.when(is_owner)
    def _():
        leave(2, k_send.at[pl.ds(0, 15)])
        leave(3, size63)
        leave(6, b2_send.at[:, pl.ds(0, 15)])
        leave(7, size63)

    @pl.when(jnp.logical_not(is_owner))
    def _():
        leave(2, k_send)
        leave(6, b2_send)


def body(pair, out_inputs, out_gate, out_final, in_inputs, in_gate, in_final):
    anywhere = pl.BlockSpec(memory_space=pl.ANY)
    return pl.pallas_call(
        kernel,
        out_shape=jax.ShapeDtypeStruct((16, 32, 128), F32),
        in_specs=[anywhere] * 7,
        out_specs=pl.BlockSpec(memory_space=pltpu.VMEM),
        scratch_shapes=[
            pltpu.VMEM((16, 32, 128), F32),
            pltpu.VMEM((2, 128, 512), BF16),
            pltpu.VMEM((2, 128, 128), BF16),
            pltpu.VMEM((2, 128, 128), BF16),
            pltpu.VMEM((16, 32, 128), BF16),
            pltpu.VMEM((2, 256, 128), BF16),
            pltpu.VMEM((2, 512, 128), BF16),
            pltpu.VMEM((2, 128, 128), BF16),
            pltpu.VMEM((2, 128, 128), BF16),
            pltpu.VMEM((2, 128, 256), F32),
            pltpu.VMEM((2, 128, 256), F32),
            pltpu.VMEM((2, 128, 256), F32),
            pltpu.VMEM((2, 128, 512), BF16),
            pltpu.VMEM((2, 8, 16, 512), BF16),
            pltpu.VMEM((4, 128, 128), F32),
            pltpu.VMEM((4, 128, 128), F32),
            pltpu.VMEM((16, 2, 32, 128), BF16),
            pltpu.VMEM((2, 2, 2, 128, 128), BF16),
            pltpu.VMEM((2, 2, 16, 16, 128), BF16),
            pltpu.VMEM((256, 128), F32),
            pltpu.VMEM((2, 16, 2, 16, 128), BF16),
            pltpu.VMEM((2, 2, 512, 512), BF16),
            pltpu.VMEM((2, 512, 256), BF16),
            pltpu.VMEM((2, 16, 16, 128), BF16),
            pltpu.VMEM((2, 16, 16, 128), BF16),
            pltpu.VMEM((2, 2, 128, 128), BF16),
            pltpu.VMEM((512, 512), BF16),
            pltpu.VMEM((16, 32, 128), BF16),
            pltpu.VMEM((4, 8, 16, 128), BF16),
            pltpu.VMEM((4, 128, 128), BF16),
            pltpu.VMEM((2, 256, 128), BF16),
            pltpu.VMEM((16, 32, 128), BF16),
            pltpu.VMEM((128, 512), F32),
            pltpu.VMEM((128, 512), F32),
            pltpu.VMEM((512, 512), BF16),
            pltpu.VMEM((1008, 256), BF16),
            pltpu.SemaphoreType.DMA((PHASES,)),
            pltpu.SemaphoreType.DMA((PHASES, 2)),
            pltpu.SemaphoreType.DMA((7,)),
            pltpu.SemaphoreType.REGULAR,
        ],
        compiler_params=pltpu.CompilerParams(
            collective_id=0, has_side_effects=True, vmem_limit_bytes=60 * 1024 * 1024
        ),
        name="triangles",
    )(pair, out_inputs, out_gate, out_final, in_inputs, in_gate, in_final)


def solution(mesh):
    placed = (P("row", "ch", None), P(), P(), P(), P(), P(), P())
    return jax.shard_map(
        body, mesh=mesh, in_specs=placed, out_specs=P("row", "ch", None), check_vma=False
    )
```
